32 devices in a mesh: pb: 8 (over z, core), pa: 4 (over y, x).
Axes of the slice: x: 2, y: 2, z: 4, core: 2. Of those that a mesh axis runs over, the one named last changes fastest.
Arguments:
- queries: bfloat16 [2560, 768], P(('pb', 'pa')), may hold values from -8 to 8
- passages: bfloat16 [2560, 768], P(('pb', 'pa')), may hold values from -8 to 8
- positives: int32 [2560], P('pb'), may hold values from 0 to 2559, each once
- inv_temp: float32 [], replicated, may hold values from 80 to 320
Outputs:
- query_loss: float32 [2560], P(('pb', 'pa'))
- query_grads: bfloat16 [2560, 768], P(('pb', 'pa'))
- passage_grads: bfloat16 [2560, 768], P(('pb', 'pa'))
The draws below stay inside these ranges and needn't reach their ends.
Inputs may be any that keep to these rules, and one draw needn't show every extreme that they name: `positives`: each passage is the positive of exactly one query.
All inputs are finite; a program needn't handle non-finite values.
Results may differ from the reference program's by a relative error of at most 0.02.
Values may be sent and summed in bfloat16 or wider, within the bound.
A program may use at most 64 MiB of HBM per device.

```python
import math
import jax
import jax.numpy as jnp
from jax import lax

D = 768
PAIRS = 2560


def draw_queries(key, part):
    key = jax.random.fold_in(key, 11)
    first = jax.random.fold_in(key, 0)
    values = jax.random.normal(first, (PAIRS, D), jnp.float32)
    return jnp.clip(values, -8.0, 8.0).astype(jnp.bfloat16)


def draw_passages(key, part):
    key = jax.random.fold_in(key, 23)
    first = jax.random.fold_in(key, 0)
    values = jax.random.normal(first, (PAIRS, D), jnp.float32)
    return jnp.clip(values, -8.0, 8.0).astype(jnp.bfloat16)


def draw_inv_temp(key, part):
    key = jax.random.fold_in(key, 37)
    return jax.random.uniform(key, (), jnp.float32, 80.0, 120.0)


def setup_inputs(seed: int = 0) -> dict:
    key_of = jax.random.split(jax.random.key(seed), 5)
    queries = draw_queries(jax.random.fold_in(key_of[4], 71), 0)
    passages = draw_passages(jax.random.fold_in(key_of[4], 71), 0)
    positives = jax.random.permutation(key_of[2], PAIRS).astype(jnp.int32)
    inv_temp = draw_inv_temp(jax.random.fold_in(key_of[4], 71), 0)
    return dict(queries=queries, passages=passages, positives=positives, inv_temp=inv_temp)


def unit_rows(values):
    wide = values.astype(jnp.float32)
    length = jnp.sqrt(lax.optimization_barrier(jnp.sum(wide * wide, axis=1, keepdims=True)))
    return (wide / length, length)

def unit_back(unit, length, grad):
    along = lax.optimization_barrier(jnp.sum(unit * grad, axis=1, keepdims=True))
    return ((grad - unit * along) / length).astype(jnp.bfloat16)

def reference(queries, passages, positives, inv_temp):
    query_unit, query_len = unit_rows(queries)
    passage_unit, passage_len = unit_rows(passages)
    query_low = query_unit.astype(jnp.bfloat16)
    passage_low = passage_unit.astype(jnp.bfloat16)
    block = math.gcd(PAIRS, 1024)
    count_blocks = PAIRS // block
    columns = jnp.arange(PAIRS, dtype=jnp.int32)

    def step(carry, inputs):
        rows, targets = inputs
        logits = jnp.dot(rows, passage_low.T, preferred_element_type=jnp.float32) * inv_temp
        total = jax.nn.logsumexp(logits, axis=1)
        hit = columns[None, :] == targets[:, None]
        positive = lax.optimization_barrier(jnp.sum(jnp.where(hit, logits, 0.0), axis=1))
        delta = (jnp.exp(logits - total[:, None]) - jnp.where(hit, 1.0, 0.0)).astype(jnp.bfloat16)
        grad_rows = inv_temp * jnp.dot(delta, passage_low, preferred_element_type=jnp.float32)
        carry = carry + inv_temp * jnp.dot(delta.T, rows, preferred_element_type=jnp.float32)
        return (carry, (total - positive, grad_rows))
    start_grad = jnp.zeros((PAIRS, D), jnp.float32)
    stacked = (query_low.reshape(count_blocks, block, D), positives.reshape(count_blocks, block))
    unit_pgrad, (losses, unit_qgrad) = lax.scan(step, start_grad, stacked)
    query_loss = losses.reshape(PAIRS)
    unit_qgrad = unit_qgrad.reshape(PAIRS, D)
    return (query_loss, unit_back(query_unit, query_len, unit_qgrad), unit_back(passage_unit, passage_len, unit_pgrad))
```

```python
import functools

import jax
import jax.numpy as jnp
from jax import lax
from jax.experimental import pallas as pl
from jax.experimental.pallas import tpu as pltpu
from jax.sharding import PartitionSpec as P

MESH = pl.DeviceIdType.MESH
F32 = jnp.float32
BF16 = jnp.bfloat16
LANES = 128
COLS = 8


def unit_rows(values):
    wide = values.astype(F32)
    length = jnp.sqrt(jnp.sum(wide * wide, axis=1, keepdims=True))
    return (wide / length, length)


def unit_back(unit, length, grad):
    along = jnp.sum(unit * grad, axis=1, keepdims=True)
    return ((grad - unit * along) / length).astype(BF16)


def repeat(count, body):
    if count <= 4:
        for k in range(count):
            body(k)
    else:

        @pl.loop(0, count)
        def _(k):
            body(k)


def kernel(
    na,
    nb,
    temp_ref,
    tgt_ref,
    q_ref,
    p_ref,
    loss_ref,
    qg_ref,
    pg_ref,
    qbuf,
    pbuf,
    tbuf,
    ebuf,
    dbuf,
    stat,
    pacc,
    psib_out,
    psib_in,
    px_out,
    px_in,
    pz_out,
    pz_in,
    qpart,
    qy_in,
    qz_out,
    qz_in,
    ps_send,
    ps_recv,
    qs_send,
    qs_recv,
    ts_send,
    ts_recv,
    ss_send,
    ss_recv,
    gp_send,
    gp_recv,
    gy_send,
    gy_recv,
    gz_send,
    gz_recv,
):
    rows = q_ref.shape[0]
    width = q_ref.shape[1]
    nr = na * nb
    pb = lax.axis_index("pb")
    pa = lax.axis_index("pa")
    zh, zl, co = pb // 4, (pb // 2) % 2, pb % 2
    yy, xx = pa // 2, pa % 2

    def dev(zh, zl, co, yy, xx):
        return (zh * 4 + zl * 2 + co, yy * 2 + xx)

    def wrap(v, n):
        return lax.rem(v, n)

    sib = dev(zh, zl, 1 - co, yy, xx)
    xnb = dev(zh, zl, co, yy, 1 - xx)
    znb = dev(zh, 1 - zl, co, yy, xx)

    def peer(dz, dy):
        return dev(wrap(zh + dz, na), zl, co, wrap(yy + dy, nb), xx)

    peers = [(dz, dy) for dz in range(na) for dy in range(nb) if dz or dy]

    barrier = pltpu.get_barrier_semaphore()
    for other in [sib, xnb, znb] + [peer(dz, dy) for dz, dy in peers]:
        pl.semaphore_signal(barrier, inc=1, device_id=other, device_id_type=MESH)

    def pslot(co, zl, xx):
        return pbuf.at[pl.ds(pl.multiple_of((co * 4 + zl * 2 + xx) * rows, 16), rows)]

    def qslot(dz, dy):
        i = wrap(zh + dz, na) * nb + wrap(yy + dy, nb)
        return qbuf.at[pl.ds(pl.multiple_of(i * LANES, LANES), rows)]

    def tslot(dz, dy):
        i = wrap(zh + dz, na) * nb + wrap(yy + dy, nb)
        return tbuf.at[i]

    def move(src, dst, send, recv, to):
        return pltpu.make_async_remote_copy(
            src_ref=src,
            dst_ref=dst,
            send_sem=send,
            recv_sem=recv,
            device_id=to,
            device_id_type=MESH,
        )

    sent = []

    def start(src, dst, send, recv, to):
        copy = move(src, dst, send, recv, to)
        copy.start()
        sent.append(copy)

    def arrive(dst, send, recv):
        move(dst, dst, send, recv, sib).wait_recv()

    p_unit, _ = unit_rows(p_ref[...])
    pslot(co, zl, xx)[...] = p_unit.astype(BF16)
    q_unit, _ = unit_rows(q_ref[...])
    qslot(0, 0)[...] = q_unit.astype(BF16)
    tslot(0, 0)[...] = tgt_ref[...]

    def clear(i):
        base = i * LANES + rows
        qbuf[pl.ds(pl.multiple_of(base, 16), LANES - rows), :] = jnp.zeros(
            (LANES - rows, width), BF16
        )

    repeat(nr, clear)
    pl.semaphore_wait(barrier, 3 + len(peers))

    def send_p(k, slot, to):
        start(slot, slot, ps_send.at[k], ps_recv.at[k], to)

    def take_p(k, slot):
        arrive(slot, ps_send.at[k], ps_recv.at[k])

    def qindex(dz, dy):
        return dz * nb + dy

    own = pslot(co, zl, xx)
    send_p(0, own, znb)
    send_p(1, own, xnb)
    mine = qslot(0, 0)
    for dz in range(1, na):
        k = qindex(dz, 0)
        start(mine, mine, qs_send.at[k], qs_recv.at[k], peer(dz, 0))
    for dy in range(1, nb):
        k = qindex(0, dy)
        start(mine, mine, qs_send.at[k], qs_recv.at[k], peer(0, dy))
    send_p(2, own, sib)
    for dz, dy in peers:
        k = qindex(dz, dy)
        start(tslot(0, 0), tslot(0, 0), ts_send.at[k], ts_recv.at[k], peer(dz, dy))

    from_z = pslot(co, 1 - zl, xx)
    take_p(0, from_z)
    send_p(3, from_z, xnb)
    send_p(4, from_z, sib)
    for dz in range(1, na):
        k = qindex(dz, 0)
        came = qslot(na - dz, 0)
        arrive(came, qs_send.at[k], qs_recv.at[k])
        for dy in range(1, nb):
            k = qindex(dz, dy)
            start(came, came, qs_send.at[k], qs_recv.at[k], peer(0, dy))
    from_x = pslot(co, zl, 1 - xx)
    take_p(1, from_x)
    send_p(5, from_x, sib)
    from_d = pslot(co, 1 - zl, 1 - xx)
    take_p(3, from_d)
    send_p(6, from_d, sib)
    for dz in range(na):
        for dy in range(1, nb):
            k = qindex(dz, dy)
            arrive(qslot((na - dz) % na, nb - dy), qs_send.at[k], qs_recv.at[k])
    for dz, dy in peers:
        k = qindex(dz, dy)
        arrive(tslot((na - dz) % na, (nb - dy) % nb), ts_send.at[k], ts_recv.at[k])
    take_p(2, pslot(1 - co, zl, xx))
    take_p(4, pslot(1 - co, 1 - zl, xx))
    take_p(5, pslot(1 - co, zl, 1 - xx))
    take_p(6, pslot(1 - co, 1 - zl, 1 - xx))

    inv_temp = temp_ref[0, 0]
    count = COLS * rows
    me_r = zh * nb + yy
    base = me_r * count
    my_stat = stat.at[me_r]

    def span(i):
        if isinstance(i, int):
            return pl.ds(i * LANES, LANES)
        return pl.ds(pl.multiple_of(i * LANES, LANES), LANES)

    def hits(i):
        target = tbuf[i][0:1, :] - base
        return lax.broadcasted_iota(jnp.int32, (count, LANES), 0) == target

    def forward(i):
        logits = (
            lax.dot_general(
                pbuf[...], qbuf[span(i), :], (((1,), (1,)), ((), ())), preferred_element_type=F32
            )
            * inv_temp
        )
        biggest = jnp.max(logits, axis=0, keepdims=True)
        powers = jnp.exp(logits - biggest)
        ebuf[:, span(i)] = powers
        my_stat[0:1, span(i)] = biggest
        my_stat[1:2, span(i)] = jnp.sum(powers, axis=0, keepdims=True)
        my_stat[2:3, span(i)] = jnp.sum(jnp.where(hits(i), logits, 0.0), axis=0, keepdims=True)

    repeat(nr, forward)

    for dz, dy in peers:
        k = qindex(dz, dy)
        start(my_stat, my_stat, ss_send.at[k], ss_recv.at[k], peer(dz, dy))
    for dz, dy in peers:
        k = qindex(dz, dy)
        i = wrap(zh + na - dz, na) * nb + wrap(yy + nb - dy, nb)
        arrive(stat.at[i], ss_send.at[k], ss_recv.at[k])

    top = stat[0, 0:1, :]
    for i in range(1, nr):
        top = jnp.maximum(top, stat[i, 0:1, :])
    summed = jnp.zeros_like(top)
    positive = jnp.zeros_like(top)
    for i in range(nr):
        summed += stat[i, 1:2, :] * jnp.exp(stat[i, 0:1, :] - top)
        positive += stat[i, 2:3, :]
    totals = top + jnp.log(summed)
    losses = totals - positive
    scale = jnp.exp(my_stat[0:1, :] - totals)
    picked = jnp.zeros((1, LANES), F32)
    for i in range(nr):
        picked = jnp.where(me_r == i, losses[:, i * LANES : (i + 1) * LANES], picked)
    loss_ref[...] = picked[:, :rows]
    stat[nr, 0:1, :] = scale

    def make_delta(i):
        part = ebuf[:, span(i)] * stat[nr, 0:1, span(i)]
        dbuf[:, span(i)] = (part - jnp.where(hits(i), 1.0, 0.0)).astype(BF16)

    repeat(nr, make_delta)

    half = count // 2

    def update(core):
        return (
            jnp.dot(
                dbuf[pl.ds(pl.multiple_of(core * half, 16), half), :],
                qbuf[...],
                preferred_element_type=F32,
            )
            * inv_temp
        )

    psib_out[...] = update(1 - co).astype(BF16)
    start(psib_out, psib_in, gp_send.at[0], gp_recv.at[0], sib)
    pacc[...] = update(co)
    arrive(psib_in, gp_send.at[0], gp_recv.at[0])

    def piece(zl, xx):
        at = pl.ds(pl.multiple_of((zl * 2 + xx) * rows, 16), rows)
        return pacc[at, :] + psib_in[at, :].astype(F32)

    px_out[0] = piece(1 - zl, 1 - xx).astype(BF16)
    start(px_out.at[0], px_in.at[0], gp_send.at[1], gp_recv.at[1], xnb)
    px_out[1] = piece(zl, 1 - xx).astype(BF16)
    start(px_out.at[1], px_in.at[1], gp_send.at[2], gp_recv.at[2], xnb)

    def query_part(i):
        part = lax.dot_general(
            dbuf[:, span(i)], pbuf[...], (((0,), (0,)), ((), ())), preferred_element_type=F32
        )
        qpart[i] = (part * inv_temp)[:rows].astype(BF16)

    repeat(nr, query_part)

    def part_at(dz, dy):
        return qpart.at[wrap(zh + dz, na) * nb + wrap(yy + dy, nb)]

    for dz in [*range(1, na), 0]:
        for dy in range(1, nb):
            k = qindex(dz, dy)
            start(part_at(dz, dy), qy_in.at[k], gy_send.at[k], gy_recv.at[k], peer(0, dy))

    arrive(px_in.at[0], gp_send.at[1], gp_recv.at[1])
    pz_out[...] = (piece(1 - zl, xx) + px_in[0].astype(F32)).astype(BF16)
    start(pz_out, pz_in, gp_send.at[3], gp_recv.at[3], znb)

    def gather_y(dz):
        total = part_at(dz, 0)[...].astype(F32)
        for dy in range(1, nb):
            k = qindex(dz, dy)
            arrive(qy_in.at[k], gy_send.at[k], gy_recv.at[k])
            total += qy_in[k].astype(F32)
        return total

    for dz in range(1, na):
        qz_out[dz] = gather_y(dz).astype(BF16)
        start(qz_out.at[dz], qz_in.at[dz], gz_send.at[dz], gz_recv.at[dz], peer(dz, 0))

    arrive(px_in.at[1], gp_send.at[2], gp_recv.at[2])
    grad = piece(zl, xx) + px_in[1].astype(F32)
    arrive(pz_in, gp_send.at[3], gp_recv.at[3])
    grad += pz_in[...].astype(F32)
    p_unit, p_len = unit_rows(p_ref[...])
    pg_ref[...] = unit_back(p_unit, p_len, grad)

    grad = gather_y(0)
    for dz in range(1, na):
        arrive(qz_in.at[dz], gz_send.at[dz], gz_recv.at[dz])
        grad += qz_in[dz].astype(F32)
    q_unit, q_len = unit_rows(q_ref[...])
    qg_ref[...] = unit_back(q_unit, q_len, grad)

    for copy in sent:
        copy.wait_send()


def local(na, nb, queries, passages, positives, inv_temp):
    rows, width = queries.shape
    nr = na * nb
    lanes = nr * LANES
    pa = lax.axis_index("pa")
    own = lax.dynamic_slice_in_dim(positives, pa * rows, rows, 0)
    shard = own // rows
    spb = shard // (nb * 2)
    spa = shard % (nb * 2)
    group = (spb // 4) * nb + spa // 2
    col = (spb % 2) * 4 + ((spb // 2) % 2) * 2 + spa % 2
    code = (group * COLS + col) * rows + own % rows
    code = jnp.pad(code.reshape(1, rows), ((0, 7), (0, LANES - rows)), constant_values=-1)
    block = (rows, width)
    vmem = pl.BlockSpec(memory_space=pltpu.VMEM)
    smem = pl.BlockSpec(memory_space=pltpu.SMEM)
    dma = pltpu.SemaphoreType.DMA
    loss, qg, pg = pl.pallas_call(
        functools.partial(kernel, na, nb),
        out_shape=(
            jax.ShapeDtypeStruct((1, rows), F32),
            jax.ShapeDtypeStruct(block, BF16),
            jax.ShapeDtypeStruct(block, BF16),
        ),
        in_specs=[smem, vmem, vmem, vmem],
        out_specs=(vmem, vmem, vmem),
        scratch_shapes=[
            pltpu.VMEM((lanes, width), BF16),
            pltpu.VMEM((COLS * rows, width), BF16),
            pltpu.VMEM((nr, 8, LANES), jnp.int32),
            pltpu.VMEM((COLS * rows, lanes), F32),
            pltpu.VMEM((COLS * rows, lanes), BF16),
            pltpu.VMEM((nr + 1, 8, lanes), F32),
            pltpu.VMEM((COLS * rows // 2, width), F32),
            pltpu.VMEM((COLS * rows // 2, width), BF16),
            pltpu.VMEM((COLS * rows // 2, width), BF16),
            pltpu.VMEM((2, *block), BF16),
            pltpu.VMEM((2, *block), BF16),
            pltpu.VMEM(block, BF16),
            pltpu.VMEM(block, BF16),
            pltpu.VMEM((nr, *block), BF16),
            pltpu.VMEM((nr, *block), BF16),
            pltpu.VMEM((na, *block), BF16),
            pltpu.VMEM((na, *block), BF16),
            dma((7,)),
            dma((7,)),
            dma((nr,)),
            dma((nr,)),
            dma((nr,)),
            dma((nr,)),
            dma((nr,)),
            dma((nr,)),
            dma((4,)),
            dma((4,)),
            dma((nr,)),
            dma((nr,)),
            dma((na,)),
            dma((na,)),
        ],
        compiler_params=pltpu.CompilerParams(
            collective_id=0, has_side_effects=True, vmem_limit_bytes=56 * 1024 * 1024
        ),
    )(inv_temp.reshape(1, 1), code, queries, passages)
    return (loss.reshape(rows), qg, pg)


def solution(mesh):
    na = mesh.shape["pb"] // 4
    nb = mesh.shape["pa"] // 2
    return jax.shard_map(
        functools.partial(local, na, nb),
        mesh=mesh,
        in_specs=(P(("pb", "pa"), None), P(("pb", "pa"), None), P("pb"), P()),
        out_specs=(P(("pb", "pa")), P(("pb", "pa"), None), P(("pb", "pa"), None)),
        check_vma=False,
    )
```

```python
import functools

import jax
import jax.numpy as jnp
from jax import lax
from jax.experimental import pallas as pl
from jax.experimental.pallas import tpu as pltpu
from jax.sharding import PartitionSpec as P

MESH = pl.DeviceIdType.MESH
F32 = jnp.float32
BF16 = jnp.bfloat16
LANES = 128
COLS = 8
STEP = 16


def unit_rows(values):
    wide = values.astype(F32)
    length = jnp.sqrt(jnp.sum(wide * wide, axis=1, keepdims=True))
    return (wide / length, length)


def unit_back(unit, length, grad):
    along = jnp.sum(unit * grad, axis=1, keepdims=True)
    return ((grad - unit * along) / length).astype(BF16)


def repeat(count, body):
    if count <= 4:
        for k in range(count):
            body(k)
    else:

        @pl.loop(0, count)
        def _(k):
            body(k)


def kernel(
    na,
    nb,
    temp_ref,
    tgt_ref,
    q_hbm,
    p_hbm,
    loss_ref,
    qg_hbm,
    pg_hbm,
    q_ref,
    p_ref,
    qg_ref,
    pg_ref,
    qbuf,
    pbuf,
    tbuf,
    ebuf,
    dbuf,
    stat,
    pacc,
    psib_out,
    psib_in,
    px_out,
    px_in,
    pz_out,
    pz_in,
    qpart,
    qy_in,
    qz_out,
    qz_in,
    io_sem,
    ps_send,
    ps_recv,
    qs_send,
    qs_recv,
    ts_send,
    ts_recv,
    ss_send,
    ss_recv,
    gs_send,
    gs_recv,
    gp_send,
    gp_recv,
    gy_send,
    gy_recv,
    gz_send,
    gz_recv,
):
    rows = q_ref.shape[0]
    width = q_ref.shape[1]
    nr = na * nb
    steps = rows // STEP
    pb = lax.axis_index("pb")
    pa = lax.axis_index("pa")
    zh, zl, co = pb // 4, (pb // 2) % 2, pb % 2
    yy, xx = pa // 2, pa % 2

    def dev(zh, zl, co, yy, xx):
        return (zh * 4 + zl * 2 + co, yy * 2 + xx)

    def wrap(v, n):
        return lax.rem(v, n)

    sib = dev(zh, zl, 1 - co, yy, xx)
    xnb = dev(zh, zl, co, yy, 1 - xx)
    znb = dev(zh, 1 - zl, co, yy, xx)

    def peer(dz, dy):
        return dev(wrap(zh + dz, na), zl, co, wrap(yy + dy, nb), xx)

    peers = [(dz, dy) for dz in range(na) for dy in range(nb) if dz or dy]

    barrier = pltpu.get_barrier_semaphore()
    for other in [sib, xnb, znb] + [peer(dz, dy) for dz, dy in peers]:
        pl.semaphore_signal(barrier, inc=1, device_id=other, device_id_type=MESH)
    load_q = pltpu.make_async_copy(q_hbm, q_ref, io_sem.at[0])
    load_p = pltpu.make_async_copy(p_hbm, p_ref, io_sem.at[1])
    load_q.start()
    load_p.start()

    def member(dz, dy):
        return wrap(zh + dz, na) * nb + wrap(yy + dy, nb)

    def pslot(co, zl, xx, h=None):
        base = (co * 4 + zl * 2 + xx) * rows
        if h is None:
            return pbuf.at[pl.ds(pl.multiple_of(base, 16), rows)]
        return pbuf.at[pl.ds(pl.multiple_of(base + h * STEP, 16), STEP)]

    def qslot(dz, dy, h=None):
        base = member(dz, dy) * LANES
        if h is None:
            return qbuf.at[pl.ds(pl.multiple_of(base, LANES), rows)]
        return qbuf.at[pl.ds(pl.multiple_of(base + h * STEP, 16), STEP)]

    def tslot(dz, dy):
        return tbuf.at[member(dz, dy)]

    def move(src, dst, send, recv, to):
        return pltpu.make_async_remote_copy(
            src_ref=src,
            dst_ref=dst,
            send_sem=send,
            recv_sem=recv,
            device_id=to,
            device_id_type=MESH,
        )

    sent = []

    def start(src, dst, send, recv, to):
        copy = move(src, dst, send, recv, to)
        copy.start()
        sent.append(copy)

    def arrive(dst, send, recv):
        move(dst, dst, send, recv, sib).wait_recv()

    def clear(i):
        base = i * LANES + rows
        qbuf[pl.ds(pl.multiple_of(base, 16), LANES - rows), :] = jnp.zeros(
            (LANES - rows, width), BF16
        )

    repeat(nr, clear)

    positives = tgt_ref[...].reshape(1, -1)
    picked = jnp.zeros((1, rows), jnp.int32)
    for k in range(nb * 2):
        picked = jnp.where(pa == k, positives[:, k * rows : (k + 1) * rows], picked)
    me_r = member(0, 0)
    tbuf[me_r] = jnp.full((8, LANES), -1, jnp.int32)
    tbuf[me_r, 0:1, 0:rows] = picked

    load_q.wait()
    q_unit, _ = unit_rows(q_ref[...])
    qslot(0, 0)[...] = q_unit.astype(BF16)
    load_p.wait()
    p_unit, _ = unit_rows(p_ref[...])
    pslot(co, zl, xx)[...] = p_unit.astype(BF16)
    pl.semaphore_wait(barrier, 3 + len(peers))

    def send_p(k, co, zl, xx, to, h=None):
        slot = pslot(co, zl, xx, h)
        at = (k, h or 0)
        start(slot, slot, ps_send.at[at], ps_recv.at[at], to)

    def take_p(k, co, zl, xx, h=None):
        at = (k, h or 0)
        arrive(pslot(co, zl, xx, h), ps_send.at[at], ps_recv.at[at])

    def send_q(dz, dy, slot, to, h=None):
        at = (dz * nb + dy, h or 0)
        start(slot, slot, qs_send.at[at], qs_recv.at[at], to)

    def take_q(dz, dy, h=None):
        at = (dz * nb + dy, h or 0)
        slot = qslot((na - dz) % na, (nb - dy) % nb, h)
        arrive(slot, qs_send.at[at], qs_recv.at[at])

    for h in range(steps):
        for dz in range(1, na):
            send_q(dz, 0, qslot(0, 0, h), peer(dz, 0), h)
        send_p(0, co, zl, xx, znb, h)
    for dy in range(1, nb):
        send_q(0, dy, qslot(0, 0), peer(0, dy))
    send_p(1, co, zl, xx, xnb)
    send_p(2, co, zl, xx, sib)
    for dz, dy in peers:
        k = dz * nb + dy
        start(tslot(0, 0), tslot(0, 0), ts_send.at[k], ts_recv.at[k], peer(dz, dy))

    for h in range(steps):
        take_p(0, co, 1 - zl, xx, h)
        send_p(3, co, 1 - zl, xx, xnb, h)
        for dz in range(1, na):
            take_q(dz, 0, h)
            for dy in range(1, nb):
                send_q(dz, dy, qslot(na - dz, 0, h), peer(0, dy), h)
    send_p(4, co, 1 - zl, xx, sib)
    take_p(1, co, zl, 1 - xx)
    send_p(5, co, zl, 1 - xx, sib)
    for h in range(steps):
        take_p(3, co, 1 - zl, 1 - xx, h)
        send_p(6, co, 1 - zl, 1 - xx, sib, h)
    for dz, dy in peers:
        k = dz * nb + dy
        arrive(tslot((na - dz) % na, (nb - dy) % nb), ts_send.at[k], ts_recv.at[k])
    take_p(2, 1 - co, zl, xx)
    take_p(4, 1 - co, 1 - zl, xx)
    take_p(5, 1 - co, zl, 1 - xx)
    for h in range(steps):
        take_p(6, 1 - co, 1 - zl, 1 - xx, h)

    inv_temp = temp_ref[0, 0]
    count = COLS * rows
    my_stat = stat.at[me_r]
    down = lax.broadcasted_iota(jnp.int32, (rows, LANES), 0)
    ids = jnp.concatenate(
        [
            down + ((zh * 4 + (j // 2) % 2 * 2 + j // 4) * (nb * 2) + yy * 2 + j % 2) * rows
            for j in range(COLS)
        ],
        axis=0,
    )

    def span(i, n=1):
        if isinstance(i, int):
            return pl.ds(i * LANES, n * LANES)
        return pl.ds(pl.multiple_of(i * LANES, LANES), n * LANES)

    def hits(i):
        return ids == tbuf[i][0:1, :]

    def forward(i):
        both = (
            lax.dot_general(
                pbuf[...],
                qbuf[span(i, 2), :],
                (((1,), (1,)), ((), ())),
                preferred_element_type=F32,
            )
            * inv_temp
        )
        for k in range(2):
            logits = both[:, k * LANES : (k + 1) * LANES]
            biggest = jnp.max(logits, axis=0, keepdims=True)
            powers = jnp.exp(logits - biggest)
            at = span(i + k)
            ebuf[:, at] = powers
            my_stat[0:1, at] = biggest
            my_stat[1:2, at] = jnp.sum(powers, axis=0, keepdims=True)
            my_stat[2:3, at] = jnp.sum(jnp.where(hits(i + k), logits, 0.0), axis=0, keepdims=True)

    for dz in range(na):
        for dy in range(1, nb):
            if dz:
                for h in range(steps):
                    take_q(dz, dy, h)
            else:
                take_q(dz, dy)
        first = wrap(zh + (na - dz), na) * nb
        repeat(nb // 2, lambda g: forward(first + g * 2))

    for dz, dy in peers:
        k = dz * nb + dy
        start(my_stat, my_stat, ss_send.at[k], ss_recv.at[k], peer(dz, dy))
    for dz, dy in peers:
        k = dz * nb + dy
        arrive(
            stat.at[member((na - dz) % na, (nb - dy) % nb)], ss_send.at[k], ss_recv.at[k]
        )

    top = stat[0, 0:1, :]
    for i in range(1, nr):
        top = jnp.maximum(top, stat[i, 0:1, :])
    summed = jnp.zeros_like(top)
    positive = jnp.zeros_like(top)
    for i in range(nr):
        summed += stat[i, 1:2, :] * jnp.exp(stat[i, 0:1, :] - top)
        positive += stat[i, 2:3, :]
    totals = top + jnp.log(summed)
    stat[nr, 0:1, :] = jnp.exp(my_stat[0:1, :] - totals)

    def make_delta(i):
        part = ebuf[:, span(i)] * stat[nr, 0:1, span(i)]
        dbuf[:, span(i)] = (part - jnp.where(hits(i), 1.0, 0.0)).astype(BF16)

    def query_part(i):
        part = lax.dot_general(
            dbuf[:, span(i, 2)], pbuf[...], (((0,), (0,)), ((), ())), preferred_element_type=F32
        )
        for k in range(2):
            qpart[i + k] = (part[k * LANES : k * LANES + rows] * inv_temp).astype(BF16)

    def part_at(dz, dy):
        return qpart.at[member(dz, dy)]

    def piece_of(ref, h):
        return ref.at[pl.ds(h * STEP, STEP)]

    for dz in [*range(1, na), 0]:
        first = wrap(zh + dz, na) * nb

        def group(g):
            make_delta(first + g * 2)
            make_delta(first + g * 2 + 1)
            query_part(first + g * 2)

        repeat(nb // 2, group)
        if dz:
            for dy in range(1, nb):
                k = dz * nb + dy
                for h in range(steps):
                    start(
                        piece_of(part_at(dz, dy), h),
                        piece_of(qy_in.at[k], h),
                        gy_send.at[k, h],
                        gy_recv.at[k, h],
                        peer(0, dy),
                    )

    half = count // 2

    def update(core):
        return (
            jnp.dot(
                dbuf[pl.ds(pl.multiple_of(core * half, 16), half), :],
                qbuf[...],
                preferred_element_type=F32,
            )
            * inv_temp
        )

    def block(ref, zl, xx):
        return ref.at[pl.ds(pl.multiple_of((zl * 2 + xx) * rows, 16), rows)]

    psib_out[...] = update(1 - co).astype(BF16)
    order = [(1, 1), (0, 1), (1, 0), (0, 0)]

    def at_order(k):
        dz, dx = order[k]
        return (1 - zl if dz else zl, 1 - xx if dx else xx)

    for k in range(4):
        start(
            block(psib_out, *at_order(k)),
            block(psib_in, *at_order(k)),
            gs_send.at[k],
            gs_recv.at[k],
            sib,
        )
    pacc[...] = update(co)

    for dz in range(1, na):
        for h in range(steps):
            total = piece_of(part_at(dz, 0), h)[...].astype(F32)
            for dy in range(1, nb):
                k = dz * nb + dy
                arrive(piece_of(qy_in.at[k], h), gy_send.at[k, h], gy_recv.at[k, h])
                total += piece_of(qy_in.at[k], h)[...].astype(F32)
            piece_of(qz_out.at[dz], h)[...] = total.astype(BF16)
            start(
                piece_of(qz_out.at[dz], h),
                piece_of(qz_in.at[dz], h),
                gz_send.at[dz, h],
                gz_recv.at[dz, h],
                peer(dz, 0),
            )
    for dy in range(1, nb):
        start(part_at(0, dy), qy_in.at[dy], gy_send.at[dy, 0], gy_recv.at[dy, 0], peer(0, dy))

    def piece(k, h=None):
        mine, came = block(pacc, *at_order(k)), block(psib_in, *at_order(k))
        if h is not None:
            mine, came = piece_of(mine, h), piece_of(came, h)
        return mine[...] + came[...].astype(F32)

    def sib_arrive(k):
        arrive(block(psib_in, *at_order(k)), gs_send.at[k], gs_recv.at[k])

    sib_arrive(0)
    px_out[0] = piece(0).astype(BF16)
    for h in range(steps):
        start(
            piece_of(px_out.at[0], h),
            piece_of(px_in.at[0], h),
            gp_send.at[0, h],
            gp_recv.at[0, h],
            xnb,
        )
    sib_arrive(1)
    px_out[1] = piece(1).astype(BF16)
    start(px_out.at[1], px_in.at[1], gp_send.at[1, 0], gp_recv.at[1, 0], xnb)
    sib_arrive(2)
    for h in range(steps):
        came = piece_of(px_in.at[0], h)
        arrive(came, gp_send.at[0, h], gp_recv.at[0, h])
        out = piece_of(pz_out, h)
        out[...] = (piece(2, h) + came[...].astype(F32)).astype(BF16)
        start(out, piece_of(pz_in, h), gp_send.at[2, h], gp_recv.at[2, h], znb)

    losses = totals - positive
    picked = jnp.zeros((1, LANES), F32)
    for i in range(nr):
        picked = jnp.where(me_r == i, losses[:, i * LANES : (i + 1) * LANES], picked)
    loss_ref[...] = picked[:, :rows]

    grad = part_at(0, 0)[...].astype(F32)
    for dy in range(1, nb):
        arrive(qy_in.at[dy], gy_send.at[dy, 0], gy_recv.at[dy, 0])
        grad += qy_in[dy].astype(F32)
    for dz in range(1, na):
        for h in range(steps):
            arrive(piece_of(qz_in.at[dz], h), gz_send.at[dz, h], gz_recv.at[dz, h])
        grad += qz_in[dz].astype(F32)
    q_unit, q_len = unit_rows(q_ref[...])
    qg_ref[...] = unit_back(q_unit, q_len, grad)
    save_q = pltpu.make_async_copy(qg_ref, qg_hbm, io_sem.at[2])
    save_q.start()

    sib_arrive(3)
    arrive(px_in.at[1], gp_send.at[1, 0], gp_recv.at[1, 0])
    grad = piece(3) + px_in[1].astype(F32)
    for h in range(steps):
        arrive(piece_of(pz_in, h), gp_send.at[2, h], gp_recv.at[2, h])
    grad += pz_in[...].astype(F32)
    p_unit, p_len = unit_rows(p_ref[...])
    pg_ref[...] = unit_back(p_unit, p_len, grad)
    save_p = pltpu.make_async_copy(pg_ref, pg_hbm, io_sem.at[3])
    save_p.start()

    for copy in sent:
        copy.wait_send()
    save_q.wait()
    save_p.wait()


def deliver(a_in, b_in, c_in, a_out, b_out, c_out, sems):
    copies = [
        pltpu.make_async_copy(src, dst, sems.at[k])
        for k, (src, dst) in enumerate([(a_in, a_out), (b_in, b_out), (c_in, c_out)])
    ]
    for copy in copies:
        copy.start()
    for copy in copies:
        copy.wait()


def local(na, nb, queries, passages, positives, inv_temp):
    rows, width = queries.shape
    nr = na * nb
    lanes = nr * LANES
    steps = rows // STEP
    block = (rows, width)
    vmem = pl.BlockSpec(memory_space=pltpu.VMEM)
    smem = pl.BlockSpec(memory_space=pltpu.SMEM)
    anywhere = pl.BlockSpec(memory_space=pl.ANY)
    dma = pltpu.SemaphoreType.DMA
    shapes = (
        jax.ShapeDtypeStruct((1, rows), F32),
        jax.ShapeDtypeStruct(block, BF16),
        jax.ShapeDtypeStruct(block, BF16),
    )
    made = pl.pallas_call(
        functools.partial(kernel, na, nb),
        out_shape=shapes,
        in_specs=[smem, vmem, anywhere, anywhere],
        out_specs=(vmem, anywhere, anywhere),
        scratch_shapes=[
            pltpu.VMEM(block, BF16),
            pltpu.VMEM(block, BF16),
            pltpu.VMEM(block, BF16),
            pltpu.VMEM(block, BF16),
            pltpu.VMEM((lanes, width), BF16),
            pltpu.VMEM((COLS * rows, width), BF16),
            pltpu.VMEM((nr, 8, LANES), jnp.int32),
            pltpu.VMEM((COLS * rows, lanes), F32),
            pltpu.VMEM((COLS * rows, lanes), BF16),
            pltpu.VMEM((nr + 1, 8, lanes), F32),
            pltpu.VMEM((COLS * rows // 2, width), F32),
            pltpu.VMEM((COLS * rows // 2, width), BF16),
            pltpu.VMEM((COLS * rows // 2, width), BF16),
            pltpu.VMEM((2, *block), BF16),
            pltpu.VMEM((2, *block), BF16),
            pltpu.VMEM(block, BF16),
            pltpu.VMEM(block, BF16),
            pltpu.VMEM((nr, *block), BF16),
            pltpu.VMEM((nr, *block), BF16),
            pltpu.VMEM((na, *block), BF16),
            pltpu.VMEM((na, *block), BF16),
            dma((4,)),
            dma((7, steps)),
            dma((7, steps)),
            dma((nr, steps)),
            dma((nr, steps)),
            dma((nr,)),
            dma((nr,)),
            dma((nr,)),
            dma((nr,)),
            dma((4,)),
            dma((4,)),
            dma((3, steps)),
            dma((3, steps)),
            dma((nr, steps)),
            dma((nr, steps)),
            dma((na, steps)),
            dma((na, steps)),
        ],
        compiler_params=pltpu.CompilerParams(
            collective_id=0, has_side_effects=True, vmem_limit_bytes=56 * 1024 * 1024
        ),
    )(inv_temp.reshape(1, 1), positives, queries, passages)
    loss, qg, pg = pl.pallas_call(
        deliver,
        out_shape=shapes,
        in_specs=[anywhere] * 3,
        out_specs=(anywhere,) * 3,
        scratch_shapes=[dma((3,))],
        compiler_params=pltpu.CompilerParams(vmem_limit_bytes=56 * 1024 * 1024),
    )(*made)
    return (loss.reshape(rows), qg, pg)


def solution(mesh):
    na = mesh.shape["pb"] // 4
    nb = mesh.shape["pa"] // 2
    return jax.shard_map(
        functools.partial(local, na, nb),
        mesh=mesh,
        in_specs=(P(("pb", "pa"), None), P(("pb", "pa"), None), P("pb"), P()),
        out_specs=(P(("pb", "pa")), P(("pb", "pa"), None), P(("pb", "pa"), None)),
        check_vma=False,
    )
```

```python
import functools

import jax
import jax.numpy as jnp
from jax import lax
from jax.experimental import pallas as pl
from jax.experimental.pallas import tpu as pltpu
from jax.sharding import PartitionSpec as P

MESH = pl.DeviceIdType.MESH
F32 = jnp.float32
BF16 = jnp.bfloat16
LANES = 128
COLS = 8


def unit_rows(values):
    wide = values.astype(F32)
    length = jnp.sqrt(jnp.sum(wide * wide, axis=1, keepdims=True))
    return (wide / length, length)


def unit_back(unit, length, grad):
    along = jnp.sum(unit * grad, axis=1, keepdims=True)
    return ((grad - unit * along) / length).astype(BF16)


def cut(rows):
    first = (rows // 2 + 15) // 16 * 16
    return [(0, first), (first, rows - first)]


def repeat(count, body):
    if count <= 4:
        for k in range(count):
            body(k)
    else:

        @pl.loop(0, count)
        def _(k):
            body(k)


def kernel(
    na,
    nb,
    temp_ref,
    tgt_ref,
    q_hbm,
    p_hbm,
    loss_ref,
    qg_hbm,
    pg_hbm,
    q_ref,
    p_ref,
    qg_ref,
    pg_ref,
    qbuf,
    pbuf,
    tbuf,
    ebuf,
    dbuf,
    stat,
    sidestat,
    pacc,
    psib_out,
    psib_in,
    px_out,
    px_in,
    pz_out,
    pz_in,
    qpart,
    qy_in,
    qz_out,
    qz_in,
    io_sem,
    ps_send,
    ps_recv,
    qs_send,
    qs_recv,
    ts_send,
    ts_recv,
    ss_send,
    ss_recv,
    gs_send,
    gs_recv,
    gp_send,
    gp_recv,
    gy_send,
    gy_recv,
    gz_send,
    gz_recv,
):
    rows = q_ref.shape[0]
    width = q_ref.shape[1]
    nr = na * nb
    pieces = cut(rows)
    steps = len(pieces)
    pb = lax.axis_index("pb")
    pa = lax.axis_index("pa")
    zh, zl, co = pb // 4, (pb // 2) % 2, pb % 2
    yy, xx = pa // 2, pa % 2

    def dev(zh, zl, co, yy, xx):
        return (zh * 4 + zl * 2 + co, yy * 2 + xx)

    def wrap(v, n):
        return lax.rem(v, n)

    sib = dev(zh, zl, 1 - co, yy, xx)
    xnb = dev(zh, zl, co, yy, 1 - xx)
    znb = dev(zh, 1 - zl, co, yy, xx)

    def peer(dz, dy):
        return dev(wrap(zh + dz, na), zl, co, wrap(yy + dy, nb), xx)

    peers = [(dz, dy) for dz in range(na) for dy in range(nb) if dz or dy]

    barrier = pltpu.get_barrier_semaphore()
    for other in [sib, xnb, znb] + [peer(dz, dy) for dz, dy in peers]:
        pl.semaphore_signal(barrier, inc=1, device_id=other, device_id_type=MESH)
    load_q = pltpu.make_async_copy(q_hbm, q_ref, io_sem.at[0])
    load_p = pltpu.make_async_copy(p_hbm, p_ref, io_sem.at[1])
    load_q.start()
    load_p.start()

    def member(dz, dy):
        return wrap(zh + dz, na) * nb + wrap(yy + dy, nb)

    def pslot(co, zl, xx, h=None):
        base = (co * 4 + zl * 2 + xx) * rows
        if h is None:
            return pbuf.at[pl.ds(pl.multiple_of(base, 16), rows)]
        return pbuf.at[pl.ds(pl.multiple_of(base + pieces[h][0], 16), pieces[h][1])]

    def qslot(dz, dy, h=None):
        base = member(dz, dy) * LANES
        if h is None:
            return qbuf.at[pl.ds(pl.multiple_of(base, LANES), rows)]
        return qbuf.at[pl.ds(pl.multiple_of(base + pieces[h][0], 16), pieces[h][1])]

    def tslot(dz, dy):
        return tbuf.at[member(dz, dy)]

    def move(src, dst, send, recv, to):
        return pltpu.make_async_remote_copy(
            src_ref=src,
            dst_ref=dst,
            send_sem=send,
            recv_sem=recv,
            device_id=to,
            device_id_type=MESH,
        )

    sent = []

    def start(src, dst, send, recv, to):
        copy = move(src, dst, send, recv, to)
        copy.start()
        sent.append(copy)

    def arrive(dst, send, recv):
        move(dst, dst, send, recv, sib).wait_recv()

    def clear(i):
        base = i * LANES + rows
        qbuf[pl.ds(pl.multiple_of(base, 16), LANES - rows), :] = jnp.zeros(
            (LANES - rows, width), BF16
        )

    repeat(nr, clear)

    positives = tgt_ref[...].reshape(1, -1)
    picked = jnp.zeros((1, rows), jnp.int32)
    for k in range(nb * 2):
        picked = jnp.where(pa == k, positives[:, k * rows : (k + 1) * rows], picked)
    me_r = member(0, 0)
    tbuf[me_r] = jnp.full((8, LANES), -1, jnp.int32)
    tbuf[me_r, 0:1, 0:rows] = picked

    load_q.wait()
    q_unit, _ = unit_rows(q_ref[...])
    qslot(0, 0)[...] = q_unit.astype(BF16)
    load_p.wait()
    p_unit, _ = unit_rows(p_ref[...])
    pslot(co, zl, xx)[...] = p_unit.astype(BF16)
    pl.semaphore_wait(barrier, 3 + len(peers))

    def send_p(k, co, zl, xx, to, h=None):
        slot = pslot(co, zl, xx, h)
        at = (k, h or 0)
        start(slot, slot, ps_send.at[at], ps_recv.at[at], to)

    def take_p(k, co, zl, xx, h=None):
        at = (k, h or 0)
        arrive(pslot(co, zl, xx, h), ps_send.at[at], ps_recv.at[at])

    def send_q(dz, dy, slot, to, h=None):
        at = (dz * nb + dy, h or 0)
        start(slot, slot, qs_send.at[at], qs_recv.at[at], to)

    def take_q(dz, dy, h=None):
        at = (dz * nb + dy, h or 0)
        slot = qslot((na - dz) % na, (nb - dy) % nb, h)
        arrive(slot, qs_send.at[at], qs_recv.at[at])

    for h in range(steps):
        for dz in range(1, na):
            send_q(dz, 0, qslot(0, 0, h), peer(dz, 0), h)
        send_p(0, co, zl, xx, znb, h)
    for dy in range(1, nb):
        send_q(0, dy, qslot(0, 0), peer(0, dy))
    send_p(1, co, zl, xx, xnb)
    send_p(2, co, zl, xx, sib)
    for dz, dy in peers:
        k = dz * nb + dy
        start(tslot(0, 0), tslot(0, 0), ts_send.at[k], ts_recv.at[k], peer(dz, dy))

    for h in range(steps):
        take_p(0, co, 1 - zl, xx, h)
        send_p(3, co, 1 - zl, xx, xnb, h)
        for dz in range(1, na):
            take_q(dz, 0, h)
            for dy in range(1, nb):
                send_q(dz, dy, qslot(na - dz, 0, h), peer(0, dy), h)
    send_p(4, co, 1 - zl, xx, sib)
    take_p(1, co, zl, 1 - xx)
    send_p(5, co, zl, 1 - xx, sib)
    for h in range(steps):
        take_p(3, co, 1 - zl, 1 - xx, h)
        send_p(6, co, 1 - zl, 1 - xx, sib, h)
    for dz, dy in peers:
        k = dz * nb + dy
        arrive(tslot((na - dz) % na, (nb - dy) % nb), ts_send.at[k], ts_recv.at[k])

    inv_temp = temp_ref[0, 0]
    count = COLS * rows
    half = count // 2
    my_stat = stat.at[me_r]
    down = lax.broadcasted_iota(jnp.int32, (rows, LANES), 0)

    def ids(core):
        blocks = [
            down + ((zh * 4 + (j // 2) * 2 + core) * (nb * 2) + yy * 2 + j % 2) * rows
            for j in range(COLS // 2)
        ]
        return jnp.concatenate(blocks, axis=0)

    own_half = pl.ds(pl.multiple_of(co * half, 16), half)
    sib_half = pl.ds(pl.multiple_of((1 - co) * half, 16), half)
    sides = [(0, own_half, ids(co)), (1, sib_half, ids(1 - co))]

    def span(i, n=1):
        if isinstance(i, int):
            return pl.ds(i * LANES, n * LANES)
        return pl.ds(pl.multiple_of(i * LANES, LANES), n * LANES)

    def forward(side, i):
        k, part, names = sides[side]
        both = (
            lax.dot_general(
                pbuf[part, :],
                qbuf[span(i, 2), :],
                (((1,), (1,)), ((), ())),
                preferred_element_type=F32,
            )
            * inv_temp
        )
        for g in range(2):
            logits = both[:, g * LANES : (g + 1) * LANES]
            biggest = jnp.max(logits, axis=0, keepdims=True)
            powers = jnp.exp(logits - biggest)
            at = span(i + g)
            ebuf[part, at] = powers
            hit = names == tbuf[i + g][0:1, :]
            sidestat[3 * k : 3 * k + 1, at] = biggest
            sidestat[3 * k + 1 : 3 * k + 2, at] = jnp.sum(powers, axis=0, keepdims=True)
            sidestat[3 * k + 2 : 3 * k + 3, at] = jnp.sum(
                jnp.where(hit, logits, 0.0), axis=0, keepdims=True
            )

    def forward_all(side, dz):
        first = wrap(zh + (na - dz), na) * nb
        repeat(nb // 2, lambda g: forward(side, first + g * 2))

    for dy in range(1, nb):
        take_q(0, dy)
    forward_all(0, 0)
    for dz in range(1, na):
        for dy in range(1, nb):
            for h in range(steps):
                take_q(dz, dy, h)
        forward_all(0, dz)
    take_p(2, 1 - co, zl, xx)
    take_p(4, 1 - co, 1 - zl, xx)
    take_p(5, 1 - co, zl, 1 - xx)
    for h in range(steps):
        take_p(6, 1 - co, 1 - zl, 1 - xx, h)
    for dz in range(na):
        forward_all(1, dz)

    top_own, top_sib = sidestat[0:1, :], sidestat[3:4, :]
    top_here = jnp.maximum(top_own, top_sib)
    my_stat[0:1, :] = top_here
    my_stat[1:2, :] = sidestat[1:2, :] * jnp.exp(top_own - top_here) + sidestat[4:5, :] * jnp.exp(
        top_sib - top_here
    )
    my_stat[2:3, :] = sidestat[2:3, :] + sidestat[5:6, :]

    for dz, dy in peers:
        k = dz * nb + dy
        start(my_stat, my_stat, ss_send.at[k], ss_recv.at[k], peer(dz, dy))
    for dz, dy in peers:
        k = dz * nb + dy
        arrive(
            stat.at[member((na - dz) % na, (nb - dy) % nb)], ss_send.at[k], ss_recv.at[k]
        )

    top = stat[0, 0:1, :]
    for i in range(1, nr):
        top = jnp.maximum(top, stat[i, 0:1, :])
    summed = jnp.zeros_like(top)
    positive = jnp.zeros_like(top)
    for i in range(nr):
        summed += stat[i, 1:2, :] * jnp.exp(stat[i, 0:1, :] - top)
        positive += stat[i, 2:3, :]
    totals = top + jnp.log(summed)
    sidestat[6:7, :] = jnp.exp(top_own - totals)
    sidestat[7:8, :] = jnp.exp(top_sib - totals)

    def make_delta(i):
        for k, part, names in sides:
            soft = ebuf[part, span(i)] * sidestat[6 + k : 7 + k, span(i)]
            hit = names == tbuf[i][0:1, :]
            dbuf[part, span(i)] = (soft - jnp.where(hit, 1.0, 0.0)).astype(BF16)

    def query_part(i):
        part = lax.dot_general(
            dbuf[:, span(i, 2)], pbuf[...], (((0,), (0,)), ((), ())), preferred_element_type=F32
        )
        for k in range(2):
            qpart[i + k] = (part[k * LANES : k * LANES + rows] * inv_temp).astype(BF16)

    def part_at(dz, dy):
        return qpart.at[member(dz, dy)]

    def piece_of(ref, h):
        return ref.at[pl.ds(*pieces[h])]

    for dz in [*range(1, na), 0]:
        first = wrap(zh + dz, na) * nb

        def group(g):
            make_delta(first + g * 2)
            make_delta(first + g * 2 + 1)
            query_part(first + g * 2)

        repeat(nb // 2, group)
        if dz:
            for dy in range(1, nb):
                k = dz * nb + dy
                for h in range(steps):
                    start(
                        piece_of(part_at(dz, dy), h),
                        piece_of(qy_in.at[k], h),
                        gy_send.at[k, h],
                        gy_recv.at[k, h],
                        peer(0, dy),
                    )

    def update(core):
        return (
            jnp.dot(
                dbuf[pl.ds(pl.multiple_of(core * half, 16), half), :],
                qbuf[...],
                preferred_element_type=F32,
            )
            * inv_temp
        )

    def block(ref, zl, xx):
        return ref.at[pl.ds(pl.multiple_of((zl * 2 + xx) * rows, 16), rows)]

    psib_out[...] = update(1 - co).astype(BF16)
    order = [(1, 1), (0, 1), (1, 0), (0, 0)]

    def at_order(k):
        dz, dx = order[k]
        return (1 - zl if dz else zl, 1 - xx if dx else xx)

    for k in range(4):
        start(
            block(psib_out, *at_order(k)),
            block(psib_in, *at_order(k)),
            gs_send.at[k],
            gs_recv.at[k],
            sib,
        )
    pacc[...] = update(co)

    for dz in range(1, na):
        for h in range(steps):
            total = piece_of(part_at(dz, 0), h)[...].astype(F32)
            for dy in range(1, nb):
                k = dz * nb + dy
                arrive(piece_of(qy_in.at[k], h), gy_send.at[k, h], gy_recv.at[k, h])
                total += piece_of(qy_in.at[k], h)[...].astype(F32)
            piece_of(qz_out.at[dz], h)[...] = total.astype(BF16)
            start(
                piece_of(qz_out.at[dz], h),
                piece_of(qz_in.at[dz], h),
                gz_send.at[dz, h],
                gz_recv.at[dz, h],
                peer(dz, 0),
            )
    for dy in range(1, nb):
        start(part_at(0, dy), qy_in.at[dy], gy_send.at[dy, 0], gy_recv.at[dy, 0], peer(0, dy))

    def piece(k, h=None):
        mine, came = block(pacc, *at_order(k)), block(psib_in, *at_order(k))
        if h is not None:
            mine, came = piece_of(mine, h), piece_of(came, h)
        return mine[...] + came[...].astype(F32)

    def sib_arrive(k):
        arrive(block(psib_in, *at_order(k)), gs_send.at[k], gs_recv.at[k])

    sib_arrive(0)
    px_out[0] = piece(0).astype(BF16)
    for h in range(steps):
        start(
            piece_of(px_out.at[0], h),
            piece_of(px_in.at[0], h),
            gp_send.at[0, h],
            gp_recv.at[0, h],
            xnb,
        )
    sib_arrive(1)
    px_out[1] = piece(1).astype(BF16)
    start(px_out.at[1], px_in.at[1], gp_send.at[1, 0], gp_recv.at[1, 0], xnb)
    sib_arrive(2)
    for h in range(steps):
        came = piece_of(px_in.at[0], h)
        arrive(came, gp_send.at[0, h], gp_recv.at[0, h])
        out = piece_of(pz_out, h)
        out[...] = (piece(2, h) + came[...].astype(F32)).astype(BF16)
        start(out, piece_of(pz_in, h), gp_send.at[2, h], gp_recv.at[2, h], znb)

    losses = totals - positive
    picked = jnp.zeros((1, LANES), F32)
    for i in range(nr):
        picked = jnp.where(me_r == i, losses[:, i * LANES : (i + 1) * LANES], picked)
    loss_ref[...] = picked[:, :rows]

    grad = part_at(0, 0)[...].astype(F32)
    for dy in range(1, nb):
        arrive(qy_in.at[dy], gy_send.at[dy, 0], gy_recv.at[dy, 0])
        grad += qy_in[dy].astype(F32)
    for dz in range(1, na):
        for h in range(steps):
            arrive(piece_of(qz_in.at[dz], h), gz_send.at[dz, h], gz_recv.at[dz, h])
        grad += qz_in[dz].astype(F32)
    q_unit, q_len = unit_rows(q_ref[...])
    qg_ref[...] = unit_back(q_unit, q_len, grad)
    save_q = pltpu.make_async_copy(qg_ref, qg_hbm, io_sem.at[2])
    save_q.start()

    sib_arrive(3)
    arrive(px_in.at[1], gp_send.at[1, 0], gp_recv.at[1, 0])
    grad = piece(3) + px_in[1].astype(F32)
    for h in range(steps):
        arrive(piece_of(pz_in, h), gp_send.at[2, h], gp_recv.at[2, h])
    grad += pz_in[...].astype(F32)
    p_unit, p_len = unit_rows(p_ref[...])
    pg_ref[...] = unit_back(p_unit, p_len, grad)
    save_p = pltpu.make_async_copy(pg_ref, pg_hbm, io_sem.at[3])
    save_p.start()

    for copy in sent:
        copy.wait_send()
    save_q.wait()
    save_p.wait()


def deliver(a_in, b_in, c_in, a_out, b_out, c_out):
    a_out[...] = a_in[...]
    b_out[...] = b_in[...]
    c_out[...] = c_in[...]


def local(na, nb, queries, passages, positives, inv_temp):
    rows, width = queries.shape
    nr = na * nb
    lanes = nr * LANES
    steps = len(cut(rows))
    block = (rows, width)
    vmem = pl.BlockSpec(memory_space=pltpu.VMEM)
    smem = pl.BlockSpec(memory_space=pltpu.SMEM)
    anywhere = pl.BlockSpec(memory_space=pl.ANY)
    dma = pltpu.SemaphoreType.DMA
    shapes = (
        jax.ShapeDtypeStruct((1, rows), F32),
        jax.ShapeDtypeStruct(block, BF16),
        jax.ShapeDtypeStruct(block, BF16),
    )
    made = pl.pallas_call(
        functools.partial(kernel, na, nb),
        out_shape=shapes,
        in_specs=[smem, vmem, anywhere, anywhere],
        out_specs=(vmem, anywhere, anywhere),
        scratch_shapes=[
            pltpu.VMEM(block, BF16),
            pltpu.VMEM(block, BF16),
            pltpu.VMEM(block, BF16),
            pltpu.VMEM(block, BF16),
            pltpu.VMEM((lanes, width), BF16),
            pltpu.VMEM((COLS * rows, width), BF16),
            pltpu.VMEM((nr, 8, LANES), jnp.int32),
            pltpu.VMEM((COLS * rows, lanes), F32),
            pltpu.VMEM((COLS * rows, lanes), BF16),
            pltpu.VMEM((nr, 8, lanes), F32),
            pltpu.VMEM((8, lanes), F32),
            pltpu.VMEM((COLS * rows // 2, width), F32),
            pltpu.VMEM((COLS * rows // 2, width), BF16),
            pltpu.VMEM((COLS * rows // 2, width), BF16),
            pltpu.VMEM((2, *block), BF16),
            pltpu.VMEM((2, *block), BF16),
            pltpu.VMEM(block, BF16),
            pltpu.VMEM(block, BF16),
            pltpu.VMEM((nr, *block), BF16),
            pltpu.VMEM((nr, *block), BF16),
            pltpu.VMEM((na, *block), BF16),
            pltpu.VMEM((na, *block), BF16),
            dma((4,)),
            dma((7, steps)),
            dma((7, steps)),
            dma((nr, steps)),
            dma((nr, steps)),
            dma((nr,)),
            dma((nr,)),
            dma((nr,)),
            dma((nr,)),
            dma((4,)),
            dma((4,)),
            dma((3, steps)),
            dma((3, steps)),
            dma((nr, steps)),
            dma((nr, steps)),
            dma((na, steps)),
            dma((na, steps)),
        ],
        compiler_params=pltpu.CompilerParams(
            collective_id=0, has_side_effects=True, vmem_limit_bytes=56 * 1024 * 1024
        ),
    )(inv_temp.reshape(1, 1), positives, queries, passages)
    loss, qg, pg = pl.pallas_call(
        deliver,
        out_shape=shapes,
        in_specs=[vmem] * 3,
        out_specs=(vmem,) * 3,
        compiler_params=pltpu.CompilerParams(vmem_limit_bytes=56 * 1024 * 1024),
    )(*made)
    return (loss.reshape(rows), qg, pg)


def solution(mesh):
    na = mesh.shape["pb"] // 4
    nb = mesh.shape["pa"] // 2
    return jax.shard_map(
        functools.partial(local, na, nb),
        mesh=mesh,
        in_specs=(P(("pb", "pa"), None), P(("pb", "pa"), None), P("pb"), P()),
        out_specs=(P(("pb", "pa")), P(("pb", "pa"), None), P(("pb", "pa"), None)),
        check_vma=False,
    )
```

```python
import functools

import jax
import jax.numpy as jnp
from jax import lax
from jax.experimental import pallas as pl
from jax.experimental.pallas import tpu as pltpu
from jax.sharding import PartitionSpec as P

MESH = pl.DeviceIdType.MESH
F32 = jnp.float32
BF16 = jnp.bfloat16
LANES = 128
COLS = 8


def unit_rows(values):
    wide = values.astype(F32)
    length = jnp.sqrt(jnp.sum(wide * wide, axis=1, keepdims=True))
    return (wide / length, length)


def unit_back(unit, length, grad):
    along = jnp.sum(unit * grad, axis=1, keepdims=True)
    return ((grad - unit * along) / length).astype(BF16)


def cut(rows):
    first = 16
    second = (rows - first) // 2 // 16 * 16
    return [(0, first), (first, second), (first + second, rows - first - second)]


def repeat(count, body):
    if count <= 4:
        for k in range(count):
            body(k)
    else:

        @pl.loop(0, count)
        def _(k):
            body(k)


def kernel(
    na,
    nb,
    temp_ref,
    tgt_ref,
    q_hbm,
    p_hbm,
    loss_ref,
    qg_hbm,
    pg_hbm,
    q_ref,
    p_ref,
    qg_ref,
    pg_ref,
    qbuf,
    pbuf,
    tbuf,
    ebuf,
    dbuf,
    stat,
    sidestat,
    pacc,
    psib_out,
    psib_in,
    px_out,
    px_in,
    pz_out,
    pz_in,
    qpart,
    qy_in,
    qz_out,
    qz_in,
    io_sem,
    ps_send,
    ps_recv,
    qs_send,
    qs_recv,
    ts_send,
    ts_recv,
    ss_send,
    ss_recv,
    gs_send,
    gs_recv,
    gp_send,
    gp_recv,
    gy_send,
    gy_recv,
    gz_send,
    gz_recv,
):
    rows = q_ref.shape[0]
    width = q_ref.shape[1]
    nr = na * nb
    pieces = cut(rows)
    steps = len(pieces)
    pb = lax.axis_index("pb")
    pa = lax.axis_index("pa")
    zh, zl, co = pb // 4, (pb // 2) % 2, pb % 2
    yy, xx = pa // 2, pa % 2

    def dev(zh, zl, co, yy, xx):
        return (zh * 4 + zl * 2 + co, yy * 2 + xx)

    def wrap(v, n):
        return lax.rem(v, n)

    sib = dev(zh, zl, 1 - co, yy, xx)
    xnb = dev(zh, zl, co, yy, 1 - xx)
    znb = dev(zh, 1 - zl, co, yy, xx)

    def peer(dz, dy):
        return dev(wrap(zh + dz, na), zl, co, wrap(yy + dy, nb), xx)

    peers = [(dz, dy) for dz in range(na) for dy in range(nb) if dz or dy]

    barrier = pltpu.get_barrier_semaphore()
    for other in [sib, xnb, znb] + [peer(dz, dy) for dz, dy in peers]:
        pl.semaphore_signal(barrier, inc=1, device_id=other, device_id_type=MESH)
    load_q = pltpu.make_async_copy(q_hbm, q_ref, io_sem.at[0])
    load_p = pltpu.make_async_copy(p_hbm, p_ref, io_sem.at[1])
    load_q.start()
    load_p.start()

    def member(dz, dy):
        return wrap(zh + dz, na) * nb + wrap(yy + dy, nb)

    def pslot(co, zl, xx, h=None):
        base = (co * 4 + xx * 2 + zl) * rows
        if h is None:
            return pbuf.at[pl.ds(pl.multiple_of(base, 16), rows)]
        return pbuf.at[pl.ds(pl.multiple_of(base + pieces[h][0], 16), pieces[h][1])]

    def qslot(dz, dy, h=None):
        base = member(dz, dy) * LANES
        if h is None:
            return qbuf.at[pl.ds(pl.multiple_of(base, LANES), rows)]
        return qbuf.at[pl.ds(pl.multiple_of(base + pieces[h][0], 16), pieces[h][1])]

    def tslot(dz, dy):
        return tbuf.at[member(dz, dy)]

    def move(src, dst, send, recv, to):
        return pltpu.make_async_remote_copy(
            src_ref=src,
            dst_ref=dst,
            send_sem=send,
            recv_sem=recv,
            device_id=to,
            device_id_type=MESH,
        )

    sent = []

    def start(src, dst, send, recv, to):
        copy = move(src, dst, send, recv, to)
        copy.start()
        sent.append(copy)

    def arrive(dst, send, recv):
        move(dst, dst, send, recv, sib).wait_recv()

    def clear(i):
        base = i * LANES + rows
        qbuf[pl.ds(pl.multiple_of(base, 16), LANES - rows), :] = jnp.zeros(
            (LANES - rows, width), BF16
        )

    repeat(nr, clear)

    positives = tgt_ref[...].reshape(1, -1)
    picked = jnp.zeros((1, rows), jnp.int32)
    for k in range(nb * 2):
        picked = jnp.where(pa == k, positives[:, k * rows : (k + 1) * rows], picked)
    me_r = member(0, 0)
    tbuf[me_r] = jnp.full((8, LANES), -1, jnp.int32)
    tbuf[me_r, 0:1, 0:rows] = picked

    load_q.wait()
    q_unit, _ = unit_rows(q_ref[...])
    qslot(0, 0)[...] = q_unit.astype(BF16)
    load_p.wait()
    p_unit, _ = unit_rows(p_ref[...])
    pslot(co, zl, xx)[...] = p_unit.astype(BF16)
    pl.semaphore_wait(barrier, 3 + len(peers))

    def send_p(k, co, zl, xx, to, h=None):
        slot = pslot(co, zl, xx, h)
        at = (k, h or 0)
        start(slot, slot, ps_send.at[at], ps_recv.at[at], to)

    def take_p(k, co, zl, xx, h=None):
        at = (k, h or 0)
        arrive(pslot(co, zl, xx, h), ps_send.at[at], ps_recv.at[at])

    def send_q(dz, dy, slot, to, h=None):
        at = (dz * nb + dy, h or 0)
        start(slot, slot, qs_send.at[at], qs_recv.at[at], to)

    def take_q(dz, dy, h=None):
        at = (dz * nb + dy, h or 0)
        slot = qslot((na - dz) % na, (nb - dy) % nb, h)
        arrive(slot, qs_send.at[at], qs_recv.at[at])

    for h in range(steps):
        for dz in range(1, na):
            send_q(dz, 0, qslot(0, 0, h), peer(dz, 0), h)
        send_p(0, co, zl, xx, znb, h)
    for dy in range(1, nb):
        send_q(0, dy, qslot(0, 0), peer(0, dy))
    send_p(1, co, zl, xx, xnb)
    send_p(2, co, zl, xx, sib)
    for dz, dy in peers:
        k = dz * nb + dy
        start(tslot(0, 0), tslot(0, 0), ts_send.at[k], ts_recv.at[k], peer(dz, dy))

    for h in range(steps):
        take_p(0, co, 1 - zl, xx, h)
        send_p(3, co, 1 - zl, xx, xnb, h)
        for dz in range(1, na):
            take_q(dz, 0, h)
            for dy in range(1, nb):
                send_q(dz, dy, qslot(na - dz, 0, h), peer(0, dy), h)
    send_p(4, co, 1 - zl, xx, sib)
    take_p(1, co, zl, 1 - xx)
    send_p(5, co, zl, 1 - xx, sib)
    for h in range(steps):
        take_p(3, co, 1 - zl, 1 - xx, h)
        send_p(6, co, 1 - zl, 1 - xx, sib, h)
    for dz, dy in peers:
        k = dz * nb + dy
        arrive(tslot((na - dz) % na, (nb - dy) % nb), ts_send.at[k], ts_recv.at[k])

    inv_temp = temp_ref[0, 0]
    count = COLS * rows
    half = count // 2
    my_stat = stat.at[me_r]
    down = lax.broadcasted_iota(jnp.int32, (rows, LANES), 0)

    def ids(core):
        blocks = [
            down + ((zh * 4 + (j % 2) * 2 + core) * (nb * 2) + yy * 2 + j // 2) * rows
            for j in range(COLS // 2)
        ]
        return jnp.concatenate(blocks, axis=0)

    own_half = pl.ds(pl.multiple_of(co * half, 16), half)
    sib_half = pl.ds(pl.multiple_of((1 - co) * half, 16), half)
    sides = [(0, own_half, ids(co)), (1, sib_half, ids(1 - co))]

    def span(i, n=1):
        if isinstance(i, int):
            return pl.ds(i * LANES, n * LANES)
        return pl.ds(pl.multiple_of(i * LANES, LANES), n * LANES)

    def forward(side, i):
        k, part, names = sides[side]
        both = (
            lax.dot_general(
                pbuf[part, :],
                qbuf[span(i, 2), :],
                (((1,), (1,)), ((), ())),
                preferred_element_type=F32,
            )
            * inv_temp
        )
        for g in range(2):
            logits = both[:, g * LANES : (g + 1) * LANES]
            biggest = jnp.max(logits, axis=0, keepdims=True)
            powers = jnp.exp(logits - biggest)
            at = span(i + g)
            ebuf[part, at] = powers
            hit = names == tbuf[i + g][0:1, :]
            sidestat[3 * k : 3 * k + 1, at] = biggest
            sidestat[3 * k + 1 : 3 * k + 2, at] = jnp.sum(powers, axis=0, keepdims=True)
            sidestat[3 * k + 2 : 3 * k + 3, at] = jnp.sum(
                jnp.where(hit, logits, 0.0), axis=0, keepdims=True
            )

    def forward_all(side, dz):
        first = wrap(zh + (na - dz), na) * nb
        repeat(nb // 2, lambda g: forward(side, first + g * 2))

    for dy in range(1, nb):
        take_q(0, dy)
    forward_all(0, 0)
    for dz in range(1, na):
        for dy in range(1, nb):
            for h in range(steps):
                take_q(dz, dy, h)
        forward_all(0, dz)
    take_p(2, 1 - co, zl, xx)
    take_p(4, 1 - co, 1 - zl, xx)
    take_p(5, 1 - co, zl, 1 - xx)
    for h in range(steps):
        take_p(6, 1 - co, 1 - zl, 1 - xx, h)
    for dz in range(na):
        forward_all(1, dz)

    top_own, top_sib = sidestat[0:1, :], sidestat[3:4, :]
    top_here = jnp.maximum(top_own, top_sib)
    my_stat[0:1, :] = top_here
    my_stat[1:2, :] = sidestat[1:2, :] * jnp.exp(top_own - top_here) + sidestat[4:5, :] * jnp.exp(
        top_sib - top_here
    )
    my_stat[2:3, :] = sidestat[2:3, :] + sidestat[5:6, :]

    for dz, dy in peers:
        k = dz * nb + dy
        start(my_stat, my_stat, ss_send.at[k], ss_recv.at[k], peer(dz, dy))
    for dz, dy in peers:
        k = dz * nb + dy
        arrive(
            stat.at[member((na - dz) % na, (nb - dy) % nb)], ss_send.at[k], ss_recv.at[k]
        )

    top = stat[0, 0:1, :]
    for i in range(1, nr):
        top = jnp.maximum(top, stat[i, 0:1, :])
    summed = jnp.zeros_like(top)
    positive = jnp.zeros_like(top)
    for i in range(nr):
        summed += stat[i, 1:2, :] * jnp.exp(stat[i, 0:1, :] - top)
        positive += stat[i, 2:3, :]
    totals = top + jnp.log(summed)
    sidestat[6:7, :] = jnp.exp(top_own - totals)
    sidestat[7:8, :] = jnp.exp(top_sib - totals)

    def make_delta(i):
        for k, part, names in sides:
            soft = ebuf[part, span(i)] * sidestat[6 + k : 7 + k, span(i)]
            hit = names == tbuf[i][0:1, :]
            dbuf[part, span(i)] = (soft - jnp.where(hit, 1.0, 0.0)).astype(BF16)

    def query_part(i):
        part = lax.dot_general(
            dbuf[:, span(i, 2)], pbuf[...], (((0,), (0,)), ((), ())), preferred_element_type=F32
        )
        for k in range(2):
            qpart[i + k] = (part[k * LANES : k * LANES + rows] * inv_temp).astype(BF16)

    def part_at(dz, dy):
        return qpart.at[member(dz, dy)]

    def piece_of(ref, h):
        return ref.at[pl.ds(*pieces[h])]

    for dz in [*range(1, na), 0]:
        first = wrap(zh + dz, na) * nb

        def group(g):
            make_delta(first + g * 2)
            make_delta(first + g * 2 + 1)
            query_part(first + g * 2)

        repeat(nb // 2, group)
        if dz:
            for dy in range(1, nb):
                k = dz * nb + dy
                for h in range(steps):
                    start(
                        piece_of(part_at(dz, dy), h),
                        piece_of(qy_in.at[k], h),
                        gy_send.at[k, h],
                        gy_recv.at[k, h],
                        peer(0, dy),
                    )

    def update(core, xx):
        base = core * half + xx * 2 * rows
        return (
            jnp.dot(
                dbuf[pl.ds(pl.multiple_of(base, 16), 2 * rows), :],
                qbuf[...],
                preferred_element_type=F32,
            )
            * inv_temp
        )

    def side(ref, xx):
        return ref.at[pl.ds(pl.multiple_of(xx * 2 * rows, 16), 2 * rows)]

    def block(ref, zl, xx):
        return ref.at[pl.ds(pl.multiple_of((xx * 2 + zl) * rows, 16), rows)]

    order = [(1, 1), (0, 1), (1, 0), (0, 0)]

    def at_order(k):
        dz, dx = order[k]
        return (1 - zl if dz else zl, 1 - xx if dx else xx)

    def to_sib(ks):
        for k in ks:
            start(
                block(psib_out, *at_order(k)),
                block(psib_in, *at_order(k)),
                gs_send.at[k],
                gs_recv.at[k],
                sib,
            )

    side(psib_out, 1 - xx)[...] = update(1 - co, 1 - xx).astype(BF16)
    to_sib([0, 1])
    side(pacc, 1 - xx)[...] = update(co, 1 - xx)

    def piece(k, h=None):
        mine, came = block(pacc, *at_order(k)), block(psib_in, *at_order(k))
        if h is not None:
            mine, came = piece_of(mine, h), piece_of(came, h)
        return mine[...] + came[...].astype(F32)

    def sib_arrive(k):
        arrive(block(psib_in, *at_order(k)), gs_send.at[k], gs_recv.at[k])

    sib_arrive(0)
    px_out[0] = piece(0).astype(BF16)
    for h in range(steps):
        start(
            piece_of(px_out.at[0], h),
            piece_of(px_in.at[0], h),
            gp_send.at[0, h],
            gp_recv.at[0, h],
            xnb,
        )
    for dz in range(1, na):
        for h in range(steps):
            total = piece_of(part_at(dz, 0), h)[...].astype(F32)
            for dy in range(1, nb):
                k = dz * nb + dy
                arrive(piece_of(qy_in.at[k], h), gy_send.at[k, h], gy_recv.at[k, h])
                total += piece_of(qy_in.at[k], h)[...].astype(F32)
            piece_of(qz_out.at[dz], h)[...] = total.astype(BF16)
            start(
                piece_of(qz_out.at[dz], h),
                piece_of(qz_in.at[dz], h),
                gz_send.at[dz, h],
                gz_recv.at[dz, h],
                peer(dz, 0),
            )
    for dy in range(1, nb):
        start(part_at(0, dy), qy_in.at[dy], gy_send.at[dy, 0], gy_recv.at[dy, 0], peer(0, dy))

    side(psib_out, xx)[...] = update(1 - co, xx).astype(BF16)
    to_sib([2, 3])
    side(pacc, xx)[...] = update(co, xx)
    sib_arrive(1)
    px_out[1] = piece(1).astype(BF16)
    sib_arrive(2)
    for h in range(steps):
        came = piece_of(px_in.at[0], h)
        arrive(came, gp_send.at[0, h], gp_recv.at[0, h])
        out = piece_of(pz_out, h)
        out[...] = (piece(2, h) + came[...].astype(F32)).astype(BF16)
        start(out, piece_of(pz_in, h), gp_send.at[2, h], gp_recv.at[2, h], znb)
        if h == steps - 2:
            start(px_out.at[1], px_in.at[1], gp_send.at[1, 0], gp_recv.at[1, 0], xnb)

    losses = totals - positive
    picked = jnp.zeros((1, LANES), F32)
    for i in range(nr):
        picked = jnp.where(me_r == i, losses[:, i * LANES : (i + 1) * LANES], picked)
    loss_ref[...] = picked[:, :rows]

    grad = part_at(0, 0)[...].astype(F32)
    for dy in range(1, nb):
        arrive(qy_in.at[dy], gy_send.at[dy, 0], gy_recv.at[dy, 0])
        grad += qy_in[dy].astype(F32)
    for dz in range(1, na):
        for h in range(steps):
            arrive(piece_of(qz_in.at[dz], h), gz_send.at[dz, h], gz_recv.at[dz, h])
        grad += qz_in[dz].astype(F32)
    q_unit, q_len = unit_rows(q_ref[...])
    qg_ref[...] = unit_back(q_unit, q_len, grad)
    save_q = pltpu.make_async_copy(qg_ref, qg_hbm, io_sem.at[2])
    save_q.start()

    sib_arrive(3)
    arrive(px_in.at[1], gp_send.at[1, 0], gp_recv.at[1, 0])
    grad = piece(3) + px_in[1].astype(F32)
    for h in range(steps):
        arrive(piece_of(pz_in, h), gp_send.at[2, h], gp_recv.at[2, h])
    grad += pz_in[...].astype(F32)
    p_unit, p_len = unit_rows(p_ref[...])
    pg_ref[...] = unit_back(p_unit, p_len, grad)
    save_p = pltpu.make_async_copy(pg_ref, pg_hbm, io_sem.at[3])
    save_p.start()

    for copy in sent:
        copy.wait_send()
    save_q.wait()
    save_p.wait()


def deliver(a_in, b_in, c_in, a_out, b_out, c_out):
    a_out[...] = a_in[...]
    b_out[...] = b_in[...]
    c_out[...] = c_in[...]


def local(na, nb, queries, passages, positives, inv_temp):
    rows, width = queries.shape
    nr = na * nb
    lanes = nr * LANES
    steps = len(cut(rows))
    block = (rows, width)
    vmem = pl.BlockSpec(memory_space=pltpu.VMEM)
    smem = pl.BlockSpec(memory_space=pltpu.SMEM)
    anywhere = pl.BlockSpec(memory_space=pl.ANY)
    dma = pltpu.SemaphoreType.DMA
    shapes = (
        jax.ShapeDtypeStruct((1, rows), F32),
        jax.ShapeDtypeStruct(block, BF16),
        jax.ShapeDtypeStruct(block, BF16),
    )
    made = pl.pallas_call(
        functools.partial(kernel, na, nb),
        out_shape=shapes,
        in_specs=[smem, vmem, anywhere, anywhere],
        out_specs=(vmem, anywhere, anywhere),
        scratch_shapes=[
            pltpu.VMEM(block, BF16),
            pltpu.VMEM(block, BF16),
            pltpu.VMEM(block, BF16),
            pltpu.VMEM(block, BF16),
            pltpu.VMEM((lanes, width), BF16),
            pltpu.VMEM((COLS * rows, width), BF16),
            pltpu.VMEM((nr, 8, LANES), jnp.int32),
            pltpu.VMEM((COLS * rows, lanes), F32),
            pltpu.VMEM((COLS * rows, lanes), BF16),
            pltpu.VMEM((nr, 8, lanes), F32),
            pltpu.VMEM((8, lanes), F32),
            pltpu.VMEM((COLS * rows // 2, width), F32),
            pltpu.VMEM((COLS * rows // 2, width), BF16),
            pltpu.VMEM((COLS * rows // 2, width), BF16),
            pltpu.VMEM((2, *block), BF16),
            pltpu.VMEM((2, *block), BF16),
            pltpu.VMEM(block, BF16),
            pltpu.VMEM(block, BF16),
            pltpu.VMEM((nr, *block), BF16),
            pltpu.VMEM((nr, *block), BF16),
            pltpu.VMEM((na, *block), BF16),
            pltpu.VMEM((na, *block), BF16),
            dma((4,)),
            dma((7, steps)),
            dma((7, steps)),
            dma((nr, steps)),
            dma((nr, steps)),
            dma((nr,)),
            dma((nr,)),
            dma((nr,)),
            dma((nr,)),
            dma((4,)),
            dma((4,)),
            dma((3, steps)),
            dma((3, steps)),
            dma((nr, steps)),
            dma((nr, steps)),
            dma((na, steps)),
            dma((na, steps)),
        ],
        compiler_params=pltpu.CompilerParams(
            collective_id=0, has_side_effects=True, vmem_limit_bytes=56 * 1024 * 1024
        ),
    )(inv_temp.reshape(1, 1), positives, queries, passages)
    loss, qg, pg = pl.pallas_call(
        deliver,
        out_shape=shapes,
        in_specs=[vmem] * 3,
        out_specs=(vmem,) * 3,
        compiler_params=pltpu.CompilerParams(vmem_limit_bytes=56 * 1024 * 1024),
    )(*made)
    return (loss.reshape(rows), qg, pg)


def solution(mesh):
    na = mesh.shape["pb"] // 4
    nb = mesh.shape["pa"] // 2
    return jax.shard_map(
        functools.partial(local, na, nb),
        mesh=mesh,
        in_specs=(P(("pb", "pa"), None), P(("pb", "pa"), None), P("pb"), P()),
        out_specs=(P(("pb", "pa")), P(("pb", "pa"), None), P(("pb", "pa"), None)),
        check_vma=False,
    )
```

```python
import functools

import jax
import jax.numpy as jnp
from jax import lax
from jax.experimental import pallas as pl
from jax.experimental.pallas import tpu as pltpu
from jax.sharding import PartitionSpec as P

MESH = pl.DeviceIdType.MESH
F32 = jnp.float32
BF16 = jnp.bfloat16
LANES = 128
COLS = 8


def unit_rows(values):
    wide = values.astype(F32)
    length = jnp.sqrt(jnp.sum(wide * wide, axis=1, keepdims=True))
    return (wide / length, length)


def unit_back(unit, length, grad):
    along = jnp.sum(unit * grad, axis=1, keepdims=True)
    return ((grad - unit * along) / length).astype(BF16)


def cut(rows):
    first = 16
    second = (rows - first) // 2 // 16 * 16
    return [(0, first), (first, second), (first + second, rows - first - second)]


def repeat(count, body):
    if count <= 4:
        for k in range(count):
            body(k)
    else:

        @pl.loop(0, count)
        def _(k):
            body(k)


def kernel(
    na,
    nb,
    temp_ref,
    tgt_ref,
    q_hbm,
    p_hbm,
    loss_ref,
    qg_hbm,
    pg_hbm,
    q_ref,
    p_ref,
    qg_ref,
    pg_ref,
    qbuf,
    pbuf,
    tbuf,
    ebuf,
    dbuf,
    stat,
    sidestat,
    colstat,
    qsoft,
    qhit,
    pacc,
    psib_out,
    psib_in,
    px_out,
    px_in,
    pz_out,
    pz_in,
    qpart,
    qy_in,
    qz_out,
    qz_in,
    io_sem,
    ps_send,
    ps_recv,
    qs_send,
    qs_recv,
    ts_send,
    ts_recv,
    ss_send,
    ss_recv,
    gs_send,
    gs_recv,
    gp_send,
    gp_recv,
    gy_send,
    gy_recv,
    gz_send,
    gz_recv,
):
    rows = q_ref.shape[0]
    width = q_ref.shape[1]
    nr = na * nb
    pieces = cut(rows)
    steps = len(pieces)
    pb = lax.axis_index("pb")
    pa = lax.axis_index("pa")
    zh, zl, co = pb // 4, (pb // 2) % 2, pb % 2
    yy, xx = pa // 2, pa % 2

    def dev(zh, zl, co, yy, xx):
        return (zh * 4 + zl * 2 + co, yy * 2 + xx)

    def wrap(v, n):
        return lax.rem(v, n)

    sib = dev(zh, zl, 1 - co, yy, xx)
    xnb = dev(zh, zl, co, yy, 1 - xx)
    znb = dev(zh, 1 - zl, co, yy, xx)

    def peer(dz, dy):
        return dev(wrap(zh + dz, na), zl, co, wrap(yy + dy, nb), xx)

    peers = [(dz, dy) for dz in range(na) for dy in range(nb) if dz or dy]

    barrier = pltpu.get_barrier_semaphore()
    for other in [sib, xnb, znb] + [peer(dz, dy) for dz, dy in peers]:
        pl.semaphore_signal(barrier, inc=1, device_id=other, device_id_type=MESH)
    load_q = pltpu.make_async_copy(q_hbm, q_ref, io_sem.at[0])
    load_p = pltpu.make_async_copy(p_hbm, p_ref, io_sem.at[1])
    load_q.start()
    load_p.start()

    def member(dz, dy):
        return wrap(zh + dz, na) * nb + wrap(yy + dy, nb)

    def pslot(co, zl, xx, h=None):
        base = (co * 4 + xx * 2 + zl) * rows
        if h is None:
            return pbuf.at[pl.ds(pl.multiple_of(base, 16), rows)]
        return pbuf.at[pl.ds(pl.multiple_of(base + pieces[h][0], 16), pieces[h][1])]

    def qslot(dz, dy, h=None):
        base = member(dz, dy) * LANES
        if h is None:
            return qbuf.at[pl.ds(pl.multiple_of(base, LANES), rows)]
        return qbuf.at[pl.ds(pl.multiple_of(base + pieces[h][0], 16), pieces[h][1])]

    def tslot(dz, dy):
        return tbuf.at[member(dz, dy)]

    def move(src, dst, send, recv, to):
        return pltpu.make_async_remote_copy(
            src_ref=src,
            dst_ref=dst,
            send_sem=send,
            recv_sem=recv,
            device_id=to,
            device_id_type=MESH,
        )

    sent = []

    def start(src, dst, send, recv, to):
        copy = move(src, dst, send, recv, to)
        copy.start()
        sent.append(copy)

    def arrive(dst, send, recv):
        move(dst, dst, send, recv, sib).wait_recv()

    def clear(i):
        base = i * LANES + rows
        qbuf[pl.ds(pl.multiple_of(base, 16), LANES - rows), :] = jnp.zeros(
            (LANES - rows, width), BF16
        )

    repeat(nr, clear)

    positives = tgt_ref[...].reshape(1, -1)
    picked = jnp.zeros((1, rows), jnp.int32)
    for k in range(nb * 2):
        picked = jnp.where(pa == k, positives[:, k * rows : (k + 1) * rows], picked)
    me_r = member(0, 0)
    tbuf[me_r] = jnp.full((8, LANES), -1, jnp.int32)
    tbuf[me_r, 0:1, 0:rows] = picked

    load_q.wait()
    q_unit, _ = unit_rows(q_ref[...])
    qslot(0, 0)[...] = q_unit.astype(BF16)
    load_p.wait()
    p_unit, _ = unit_rows(p_ref[...])
    pslot(co, zl, xx)[...] = p_unit.astype(BF16)
    pl.semaphore_wait(barrier, 3 + len(peers))

    def send_p(k, co, zl, xx, to, h=None):
        slot = pslot(co, zl, xx, h)
        at = (k, h or 0)
        start(slot, slot, ps_send.at[at], ps_recv.at[at], to)

    def take_p(k, co, zl, xx, h=None):
        at = (k, h or 0)
        arrive(pslot(co, zl, xx, h), ps_send.at[at], ps_recv.at[at])

    def send_q(dz, dy, slot, to, h=None):
        at = (dz * nb + dy, h or 0)
        start(slot, slot, qs_send.at[at], qs_recv.at[at], to)

    def take_q(dz, dy, h=None):
        at = (dz * nb + dy, h or 0)
        slot = qslot((na - dz) % na, (nb - dy) % nb, h)
        arrive(slot, qs_send.at[at], qs_recv.at[at])

    for h in range(steps):
        for dz in range(1, na):
            send_q(dz, 0, qslot(0, 0, h), peer(dz, 0), h)
        send_p(0, co, zl, xx, znb, h)
    for dy in range(1, nb):
        send_q(0, dy, qslot(0, 0), peer(0, dy))
    send_p(1, co, zl, xx, xnb)
    send_p(2, co, zl, xx, sib)
    for dz, dy in peers:
        k = dz * nb + dy
        start(tslot(0, 0), tslot(0, 0), ts_send.at[k], ts_recv.at[k], peer(dz, dy))

    for h in range(steps):
        take_p(0, co, 1 - zl, xx, h)
        send_p(3, co, 1 - zl, xx, xnb, h)
        for dz in range(1, na):
            take_q(dz, 0, h)
            for dy in range(1, nb):
                send_q(dz, dy, qslot(na - dz, 0, h), peer(0, dy), h)
    send_p(4, co, 1 - zl, xx, sib)
    take_p(1, co, zl, 1 - xx)
    send_p(5, co, zl, 1 - xx, sib)
    for h in range(steps):
        take_p(3, co, 1 - zl, 1 - xx, h)
        send_p(6, co, 1 - zl, 1 - xx, sib, h)
    for dz, dy in peers:
        k = dz * nb + dy
        arrive(tslot((na - dz) % na, (nb - dy) % nb), ts_send.at[k], ts_recv.at[k])

    inv_temp = temp_ref[0, 0]
    count = COLS * rows
    half = count // 2
    my_stat = stat.at[me_r]
    down = lax.broadcasted_iota(jnp.int32, (rows, LANES), 0)

    def ids(core):
        blocks = [
            down + ((zh * 4 + (j % 2) * 2 + core) * (nb * 2) + yy * 2 + j // 2) * rows
            for j in range(COLS // 2)
        ]
        return jnp.concatenate(blocks, axis=0)

    own_half = pl.ds(pl.multiple_of(co * half, 16), half)
    sib_half = pl.ds(pl.multiple_of((1 - co) * half, 16), half)
    sides = [(0, own_half, ids(co)), (1, sib_half, ids(1 - co))]

    def span(i, n=1):
        if isinstance(i, int):
            return pl.ds(i * LANES, n * LANES)
        return pl.ds(pl.multiple_of(i * LANES, LANES), n * LANES)

    def forward(side, i):
        k, part, names = sides[side]
        both = (
            lax.dot_general(
                pbuf[part, :],
                qbuf[span(i, 2), :],
                (((1,), (1,)), ((), ())),
                preferred_element_type=F32,
            )
            * inv_temp
        )
        for g in range(2):
            logits = both[:, g * LANES : (g + 1) * LANES]
            biggest = jnp.max(logits, axis=0, keepdims=True)
            powers = jnp.exp(logits - biggest)
            at = span(i + g)
            ebuf[part, at] = powers
            hit = names == tbuf[i + g][0:1, :]
            sidestat[3 * k : 3 * k + 1, at] = biggest
            sidestat[3 * k + 1 : 3 * k + 2, at] = jnp.sum(powers, axis=0, keepdims=True)
            sidestat[3 * k + 2 : 3 * k + 3, at] = jnp.sum(
                jnp.where(hit, logits, 0.0), axis=0, keepdims=True
            )

    def forward_all(side, dz):
        first = wrap(zh + (na - dz), na) * nb
        repeat(nb // 2, lambda g: forward(side, first + g * 2))

    for dy in range(1, nb):
        take_q(0, dy)
    forward_all(0, 0)
    for dz in range(1, na):
        for dy in range(1, nb):
            for h in range(steps):
                take_q(dz, dy, h)
        forward_all(0, dz)
    take_p(2, 1 - co, zl, xx)
    take_p(4, 1 - co, 1 - zl, xx)
    take_p(5, 1 - co, zl, 1 - xx)
    for h in range(steps):
        take_p(6, 1 - co, 1 - zl, 1 - xx, h)
    for dz in range(na):
        forward_all(1, dz)

    top_own, top_sib = sidestat[0:1, :], sidestat[3:4, :]
    top_here = jnp.maximum(top_own, top_sib)
    my_stat[0:1, :] = top_here
    my_stat[1:2, :] = sidestat[1:2, :] * jnp.exp(top_own - top_here) + sidestat[4:5, :] * jnp.exp(
        top_sib - top_here
    )
    my_stat[2:3, :] = sidestat[2:3, :] + sidestat[5:6, :]

    for dz, dy in peers:
        k = dz * nb + dy
        start(my_stat, my_stat, ss_send.at[k], ss_recv.at[k], peer(dz, dy))

    for k, top in enumerate([top_own, top_sib]):
        colstat[k : k + 1, :] = jnp.exp(top - top_here)

    def query_part(i):
        parts = jnp.zeros((4 * LANES, width), F32)
        for k, part, names in sides:
            softs, picks = [], []
            for g in range(2):
                at = span(i + g)
                hit = names == tbuf[i + g][0:1, :]
                soft = ebuf[part, at] * colstat[k : k + 1, at]
                softs.append(jnp.where(hit, 0.0, soft).astype(BF16))
                picks.append(jnp.where(hit, 1.0, 0.0).astype(BF16))
            parts += lax.dot_general(
                jnp.concatenate(softs + picks, axis=1),
                pbuf[part, :],
                (((0,), (0,)), ((), ())),
                preferred_element_type=F32,
            )
        for g in range(2):
            qsoft[i + g] = parts[g * LANES : g * LANES + rows].astype(BF16)
            qhit[i + g] = parts[(2 + g) * LANES : (2 + g) * LANES + rows].astype(BF16)

    repeat(nr // 2, lambda g: query_part(g * 2))

    for dz, dy in peers:
        k = dz * nb + dy
        arrive(
            stat.at[member((na - dz) % na, (nb - dy) % nb)], ss_send.at[k], ss_recv.at[k]
        )

    top = stat[0, 0:1, :]
    for i in range(1, nr):
        top = jnp.maximum(top, stat[i, 0:1, :])
    summed = jnp.zeros_like(top)
    positive = jnp.zeros_like(top)
    for i in range(nr):
        summed += stat[i, 1:2, :] * jnp.exp(stat[i, 0:1, :] - top)
        positive += stat[i, 2:3, :]
    totals = top + jnp.log(summed)
    sidestat[6:7, :] = jnp.exp(top_own - totals)
    sidestat[7:8, :] = jnp.exp(top_sib - totals)

    colstat[0:1, :] = jnp.exp(top_here - totals)
    colstat[1:2, :] = jnp.exp(positive - totals) - 1.0

    def query_scale(i):
        factors = jnp.transpose(colstat[:, span(i)])[:rows]
        part = qsoft[i].astype(F32) * factors[:, 0:1] + qhit[i].astype(F32) * factors[:, 1:2]
        qpart[i] = (part * inv_temp).astype(BF16)

    def part_at(dz, dy):
        return qpart.at[member(dz, dy)]

    def piece_of(ref, h):
        return ref.at[pl.ds(*pieces[h])]

    for dz in range(1, na):
        first = wrap(zh + dz, na) * nb

        repeat(nb, lambda g: query_scale(first + g))
        for dy in range(1, nb):
            k = dz * nb + dy
            for h in range(steps):
                start(
                    piece_of(part_at(dz, dy), h),
                    piece_of(qy_in.at[k], h),
                    gy_send.at[k, h],
                    gy_recv.at[k, h],
                    peer(0, dy),
                )

    def update(k, xx):
        core = 1 - co if k else co
        base = core * half + xx * 2 * rows
        part = pl.ds(pl.multiple_of(base, 16), 2 * rows)
        names = jnp.concatenate(
            [down + ((zh * 4 + j * 2 + core) * (nb * 2) + yy * 2 + xx) * rows for j in range(2)],
            axis=0,
        )

        def make_delta(i):
            soft = ebuf[part, span(i)] * sidestat[6 + k : 7 + k, span(i)]
            hit = names == tbuf[i][0:1, :]
            dbuf[part, span(i)] = (soft - jnp.where(hit, 1.0, 0.0)).astype(BF16)

        repeat(nr, make_delta)
        return (
            jnp.dot(
                dbuf[part, :],
                qbuf[...],
                preferred_element_type=F32,
            )
            * inv_temp
        )

    def side(ref, xx):
        return ref.at[pl.ds(pl.multiple_of(xx * 2 * rows, 16), 2 * rows)]

    def block(ref, zl, xx):
        return ref.at[pl.ds(pl.multiple_of((xx * 2 + zl) * rows, 16), rows)]

    order = [(1, 1), (0, 1), (1, 0), (0, 0)]

    def at_order(k):
        dz, dx = order[k]
        return (1 - zl if dz else zl, 1 - xx if dx else xx)

    def to_sib(ks):
        for k in ks:
            start(
                block(psib_out, *at_order(k)),
                block(psib_in, *at_order(k)),
                gs_send.at[k],
                gs_recv.at[k],
                sib,
            )

    side(psib_out, 1 - xx)[...] = update(1, 1 - xx).astype(BF16)
    to_sib([0, 1])
    side(pacc, 1 - xx)[...] = update(0, 1 - xx)

    def piece(k, h=None):
        mine, came = block(pacc, *at_order(k)), block(psib_in, *at_order(k))
        if h is not None:
            mine, came = piece_of(mine, h), piece_of(came, h)
        return mine[...] + came[...].astype(F32)

    def sib_arrive(k):
        arrive(block(psib_in, *at_order(k)), gs_send.at[k], gs_recv.at[k])

    sib_arrive(0)
    px_out[0] = piece(0).astype(BF16)
    for h in range(steps):
        start(
            piece_of(px_out.at[0], h),
            piece_of(px_in.at[0], h),
            gp_send.at[0, h],
            gp_recv.at[0, h],
            xnb,
        )
    for dz in range(1, na):
        for h in range(steps):
            total = piece_of(part_at(dz, 0), h)[...].astype(F32)
            for dy in range(1, nb):
                k = dz * nb + dy
                arrive(piece_of(qy_in.at[k], h), gy_send.at[k, h], gy_recv.at[k, h])
                total += piece_of(qy_in.at[k], h)[...].astype(F32)
            piece_of(qz_out.at[dz], h)[...] = total.astype(BF16)
            start(
                piece_of(qz_out.at[dz], h),
                piece_of(qz_in.at[dz], h),
                gz_send.at[dz, h],
                gz_recv.at[dz, h],
                peer(dz, 0),
            )
    repeat(nb, lambda g: query_scale(zh * nb + g))
    for dy in range(1, nb):
        start(part_at(0, dy), qy_in.at[dy], gy_send.at[dy, 0], gy_recv.at[dy, 0], peer(0, dy))

    side(psib_out, xx)[...] = update(1, xx).astype(BF16)
    to_sib([2, 3])
    side(pacc, xx)[...] = update(0, xx)
    sib_arrive(1)
    px_out[1] = piece(1).astype(BF16)
    sib_arrive(2)
    for h in range(steps):
        came = piece_of(px_in.at[0], h)
        arrive(came, gp_send.at[0, h], gp_recv.at[0, h])
        out = piece_of(pz_out, h)
        out[...] = (piece(2, h) + came[...].astype(F32)).astype(BF16)
        start(out, piece_of(pz_in, h), gp_send.at[2, h], gp_recv.at[2, h], znb)
        if h == 0:
            start(px_out.at[1], px_in.at[1], gp_send.at[1, 0], gp_recv.at[1, 0], xnb)

    losses = totals - positive
    picked = jnp.zeros((1, LANES), F32)
    for i in range(nr):
        picked = jnp.where(me_r == i, losses[:, i * LANES : (i + 1) * LANES], picked)
    loss_ref[...] = picked[:, :rows]

    grad = part_at(0, 0)[...].astype(F32)
    for dy in range(1, nb):
        arrive(qy_in.at[dy], gy_send.at[dy, 0], gy_recv.at[dy, 0])
        grad += qy_in[dy].astype(F32)
    for dz in range(1, na):
        for h in range(steps):
            arrive(piece_of(qz_in.at[dz], h), gz_send.at[dz, h], gz_recv.at[dz, h])
        grad += qz_in[dz].astype(F32)
    q_unit, q_len = unit_rows(q_ref[...])
    qg_ref[...] = unit_back(q_unit, q_len, grad)
    save_q = pltpu.make_async_copy(qg_ref, qg_hbm, io_sem.at[2])
    save_q.start()

    sib_arrive(3)
    arrive(px_in.at[1], gp_send.at[1, 0], gp_recv.at[1, 0])
    grad = piece(3) + px_in[1].astype(F32)
    for h in range(steps):
        arrive(piece_of(pz_in, h), gp_send.at[2, h], gp_recv.at[2, h])
    grad += pz_in[...].astype(F32)
    p_unit, p_len = unit_rows(p_ref[...])
    pg_ref[...] = unit_back(p_unit, p_len, grad)
    save_p = pltpu.make_async_copy(pg_ref, pg_hbm, io_sem.at[3])
    save_p.start()

    for copy in sent:
        copy.wait_send()
    save_q.wait()
    save_p.wait()


def deliver(a_in, b_in, c_in, a_out, b_out, c_out):
    a_out[...] = a_in[...]
    b_out[...] = b_in[...]
    c_out[...] = c_in[...]


def local(na, nb, queries, passages, positives, inv_temp):
    rows, width = queries.shape
    nr = na * nb
    lanes = nr * LANES
    steps = len(cut(rows))
    block = (rows, width)
    vmem = pl.BlockSpec(memory_space=pltpu.VMEM)
    smem = pl.BlockSpec(memory_space=pltpu.SMEM)
    anywhere = pl.BlockSpec(memory_space=pl.ANY)
    dma = pltpu.SemaphoreType.DMA
    shapes = (
        jax.ShapeDtypeStruct((1, rows), F32),
        jax.ShapeDtypeStruct(block, BF16),
        jax.ShapeDtypeStruct(block, BF16),
    )
    made = pl.pallas_call(
        functools.partial(kernel, na, nb),
        out_shape=shapes,
        in_specs=[smem, vmem, anywhere, anywhere],
        out_specs=(vmem, anywhere, anywhere),
        scratch_shapes=[
            pltpu.VMEM(block, BF16),
            pltpu.VMEM(block, BF16),
            pltpu.VMEM(block, BF16),
            pltpu.VMEM(block, BF16),
            pltpu.VMEM((lanes, width), BF16),
            pltpu.VMEM((COLS * rows, width), BF16),
            pltpu.VMEM((nr, 8, LANES), jnp.int32),
            pltpu.VMEM((COLS * rows, lanes), F32),
            pltpu.VMEM((COLS * rows, lanes), BF16),
            pltpu.VMEM((nr, 8, lanes), F32),
            pltpu.VMEM((8, lanes), F32),
            pltpu.VMEM((8, lanes), F32),
            pltpu.VMEM((nr, *block), BF16),
            pltpu.VMEM((nr, *block), BF16),
            pltpu.VMEM((COLS * rows // 2, width), F32),
            pltpu.VMEM((COLS * rows // 2, width), BF16),
            pltpu.VMEM((COLS * rows // 2, width), BF16),
            pltpu.VMEM((2, *block), BF16),
            pltpu.VMEM((2, *block), BF16),
            pltpu.VMEM(block, BF16),
            pltpu.VMEM(block, BF16),
            pltpu.VMEM((nr, *block), BF16),
            pltpu.VMEM((nr, *block), BF16),
            pltpu.VMEM((na, *block), BF16),
            pltpu.VMEM((na, *block), BF16),
            dma((4,)),
            dma((7, steps)),
            dma((7, steps)),
            dma((nr, steps)),
            dma((nr, steps)),
            dma((nr,)),
            dma((nr,)),
            dma((nr,)),
            dma((nr,)),
            dma((4,)),
            dma((4,)),
            dma((3, steps)),
            dma((3, steps)),
            dma((nr, steps)),
            dma((nr, steps)),
            dma((na, steps)),
            dma((na, steps)),
        ],
        compiler_params=pltpu.CompilerParams(
            collective_id=0, has_side_effects=True, vmem_limit_bytes=56 * 1024 * 1024
        ),
    )(inv_temp.reshape(1, 1), positives, queries, passages)
    loss, qg, pg = pl.pallas_call(
        deliver,
        out_shape=shapes,
        in_specs=[vmem] * 3,
        out_specs=(vmem,) * 3,
        compiler_params=pltpu.CompilerParams(vmem_limit_bytes=56 * 1024 * 1024),
    )(*made)
    return (loss.reshape(rows), qg, pg)


def solution(mesh):
    na = mesh.shape["pb"] // 4
    nb = mesh.shape["pa"] // 2
    return jax.shard_map(
        functools.partial(local, na, nb),
        mesh=mesh,
        in_specs=(P(("pb", "pa"), None), P(("pb", "pa"), None), P("pb"), P()),
        out_specs=(P(("pb", "pa")), P(("pb", "pa"), None), P(("pb", "pa"), None)),
        check_vma=False,
    )
```

```python
import functools

import jax
import jax.numpy as jnp
from jax import lax
from jax.experimental import pallas as pl
from jax.experimental.pallas import tpu as pltpu
from jax.sharding import PartitionSpec as P

MESH = pl.DeviceIdType.MESH
F32 = jnp.float32
BF16 = jnp.bfloat16
LANES = 128
COLS = 8


def unit_rows(values):
    wide = values.astype(F32)
    length = jnp.sqrt(jnp.sum(wide * wide, axis=1, keepdims=True))
    return (wide / length, length)


def unit_back(unit, length, grad):
    along = jnp.sum(unit * grad, axis=1, keepdims=True)
    return ((grad - unit * along) / length).astype(BF16)


def cut(rows):
    first = 16
    second = (rows - first) // 2 // 16 * 16
    return [(0, first), (first, second), (first + second, rows - first - second)]


def repeat(count, body):
    if count <= 4:
        for k in range(count):
            body(k)
    else:

        @pl.loop(0, count)
        def _(k):
            body(k)


def kernel(
    na,
    nb,
    temp_ref,
    tgt_ref,
    q_hbm,
    p_hbm,
    loss_ref,
    qg_hbm,
    pg_hbm,
    q_ref,
    p_ref,
    qg_ref,
    pg_ref,
    qbuf,
    pbuf,
    tbuf,
    ebuf,
    dbuf,
    stat,
    sidestat,
    colstat,
    qsoft,
    qhit,
    pacc,
    psib_out,
    psib_in,
    px_out,
    px_in,
    pz_out,
    pz_in,
    qpart,
    qy_in,
    qz_out,
    qz_in,
    io_sem,
    ps_send,
    ps_recv,
    qs_send,
    qs_recv,
    ts_send,
    ts_recv,
    ss_send,
    ss_recv,
    gs_send,
    gs_recv,
    gp_send,
    gp_recv,
    gy_send,
    gy_recv,
    gz_send,
    gz_recv,
):
    rows = q_ref.shape[0]
    width = q_ref.shape[1]
    nr = na * nb
    pieces = cut(rows)
    steps = len(pieces)
    pb = lax.axis_index("pb")
    pa = lax.axis_index("pa")
    zh, zl, co = pb // 4, (pb // 2) % 2, pb % 2
    yy, xx = pa // 2, pa % 2

    def dev(zh, zl, co, yy, xx):
        return (zh * 4 + zl * 2 + co, yy * 2 + xx)

    def wrap(v, n):
        return lax.rem(v, n)

    sib = dev(zh, zl, 1 - co, yy, xx)
    xnb = dev(zh, zl, co, yy, 1 - xx)
    znb = dev(zh, 1 - zl, co, yy, xx)

    def peer(dz, dy):
        return dev(wrap(zh + dz, na), zl, co, wrap(yy + dy, nb), xx)

    peers = [(dz, dy) for dz in range(na) for dy in range(nb) if dz or dy]

    barrier = pltpu.get_barrier_semaphore()
    for other in [sib, xnb, znb] + [peer(dz, dy) for dz, dy in peers]:
        pl.semaphore_signal(barrier, inc=1, device_id=other, device_id_type=MESH)
    load_q = pltpu.make_async_copy(q_hbm, q_ref, io_sem.at[0])
    load_p = pltpu.make_async_copy(p_hbm, p_ref, io_sem.at[1])
    load_q.start()
    load_p.start()

    def member(dz, dy):
        return wrap(zh + dz, na) * nb + wrap(yy + dy, nb)

    def pslot(far, zl, xx, h=None):
        base = (far * 4 + xx * 2 + zl) * rows
        if h is None:
            return pbuf.at[pl.ds(pl.multiple_of(base, 16), rows)]
        return pbuf.at[pl.ds(pl.multiple_of(base + pieces[h][0], 16), pieces[h][1])]

    def qslot(dz, dy, h=None):
        base = member(dz, dy) * LANES
        if h is None:
            return qbuf.at[pl.ds(pl.multiple_of(base, LANES), rows)]
        return qbuf.at[pl.ds(pl.multiple_of(base + pieces[h][0], 16), pieces[h][1])]

    def tslot(dz, dy):
        return tbuf.at[member(dz, dy)]

    def move(src, dst, send, recv, to):
        return pltpu.make_async_remote_copy(
            src_ref=src,
            dst_ref=dst,
            send_sem=send,
            recv_sem=recv,
            device_id=to,
            device_id_type=MESH,
        )

    sent = []

    def start(src, dst, send, recv, to):
        copy = move(src, dst, send, recv, to)
        copy.start()
        sent.append(copy)

    def arrive(dst, send, recv):
        move(dst, dst, send, recv, sib).wait_recv()

    def clear(i):
        base = i * LANES + rows
        qbuf[pl.ds(pl.multiple_of(base, 16), LANES - rows), :] = jnp.zeros(
            (LANES - rows, width), BF16
        )

    repeat(nr, clear)

    positives = tgt_ref[...].reshape(1, -1)
    picked = jnp.zeros((1, rows), jnp.int32)
    for k in range(nb * 2):
        picked = jnp.where(pa == k, positives[:, k * rows : (k + 1) * rows], picked)
    me_r = member(0, 0)
    tbuf[me_r] = jnp.full((8, LANES), -1, jnp.int32)
    tbuf[me_r, 0:1, 0:rows] = picked

    load_q.wait()
    q_unit, _ = unit_rows(q_ref[...])
    qslot(0, 0)[...] = q_unit.astype(BF16)
    load_p.wait()
    p_unit, _ = unit_rows(p_ref[...])
    pslot(0, zl, xx)[...] = p_unit.astype(BF16)
    pl.semaphore_wait(barrier, 3 + len(peers))

    def send_p(k, zl, xx, to, h=None):
        far = 1 if k in (2, 4, 5, 6) else 0
        at = (k, h or 0)
        start(pslot(0, zl, xx, h), pslot(far, zl, xx, h), ps_send.at[at], ps_recv.at[at], to)

    def take_p(k, zl, xx, h=None):
        far = 1 if k in (2, 4, 5, 6) else 0
        at = (k, h or 0)
        arrive(pslot(far, zl, xx, h), ps_send.at[at], ps_recv.at[at])

    def send_q(dz, dy, slot, to, h=None):
        at = (dz * nb + dy, h or 0)
        start(slot, slot, qs_send.at[at], qs_recv.at[at], to)

    def take_q(dz, dy, h=None):
        at = (dz * nb + dy, h or 0)
        slot = qslot((na - dz) % na, (nb - dy) % nb, h)
        arrive(slot, qs_send.at[at], qs_recv.at[at])

    for h in range(steps):
        for dz in range(1, na):
            send_q(dz, 0, qslot(0, 0, h), peer(dz, 0), h)
        send_p(0, zl, xx, znb, h)
    for dy in range(1, nb):
        send_q(0, dy, qslot(0, 0), peer(0, dy))
    send_p(1, zl, xx, xnb)
    send_p(2, zl, xx, sib)
    for dz, dy in peers:
        k = dz * nb + dy
        start(tslot(0, 0), tslot(0, 0), ts_send.at[k], ts_recv.at[k], peer(dz, dy))

    for h in range(steps):
        take_p(0, 1 - zl, xx, h)
        send_p(3, 1 - zl, xx, xnb, h)
        for dz in range(1, na):
            take_q(dz, 0, h)
            for dy in range(1, nb):
                send_q(dz, dy, qslot(na - dz, 0, h), peer(0, dy), h)
    send_p(4, 1 - zl, xx, sib)
    take_p(1, zl, 1 - xx)
    send_p(5, zl, 1 - xx, sib)
    for h in range(steps):
        take_p(3, 1 - zl, 1 - xx, h)
        send_p(6, 1 - zl, 1 - xx, sib, h)
    for dz, dy in peers:
        k = dz * nb + dy
        arrive(tslot((na - dz) % na, (nb - dy) % nb), ts_send.at[k], ts_recv.at[k])

    inv_temp = temp_ref[0, 0]
    count = COLS * rows
    half = count // 2
    my_stat = stat.at[me_r]
    down = lax.broadcasted_iota(jnp.int32, (rows, LANES), 0)

    def ids(core):
        blocks = [
            down + ((zh * 4 + (j % 2) * 2 + core) * (nb * 2) + yy * 2 + j // 2) * rows
            for j in range(COLS // 2)
        ]
        return jnp.concatenate(blocks, axis=0)

    own_half = pl.ds(0, half)
    sib_half = pl.ds(half, half)
    sides = [(0, own_half, ids(co)), (1, sib_half, ids(1 - co))]

    def span(i, n=1):
        if isinstance(i, int):
            return pl.ds(i * LANES, n * LANES)
        return pl.ds(pl.multiple_of(i * LANES, LANES), n * LANES)

    def forward(side, i):
        k, part, names = sides[side]
        both = (
            lax.dot_general(
                pbuf[part, :],
                qbuf[span(i, 2), :],
                (((1,), (1,)), ((), ())),
                preferred_element_type=F32,
            )
            * inv_temp
        )
        for g in range(2):
            logits = both[:, g * LANES : (g + 1) * LANES]
            biggest = jnp.max(logits, axis=0, keepdims=True)
            powers = jnp.exp(logits - biggest)
            at = span(i + g)
            ebuf[part, at] = powers
            hit = names == tbuf[i + g][0:1, :]
            sidestat[3 * k : 3 * k + 1, at] = biggest
            sidestat[3 * k + 1 : 3 * k + 2, at] = jnp.sum(powers, axis=0, keepdims=True)
            sidestat[3 * k + 2 : 3 * k + 3, at] = jnp.sum(
                jnp.where(hit, logits, 0.0), axis=0, keepdims=True
            )

    def forward_all(side, dz):
        first = wrap(zh + (na - dz), na) * nb
        repeat(nb // 2, lambda g: forward(side, first + g * 2))

    for dy in range(1, nb):
        take_q(0, dy)
    forward_all(0, 0)
    for dz in range(1, na):
        for dy in range(1, nb):
            for h in range(steps):
                take_q(dz, dy, h)
        forward_all(0, dz)
    take_p(2, zl, xx)
    take_p(4, 1 - zl, xx)
    take_p(5, zl, 1 - xx)
    for h in range(steps):
        take_p(6, 1 - zl, 1 - xx, h)
    for dz in range(na):
        forward_all(1, dz)

    top_own, top_sib = sidestat[0:1, :], sidestat[3:4, :]
    top_here = jnp.maximum(top_own, top_sib)
    my_stat[0:1, :] = top_here
    my_stat[1:2, :] = sidestat[1:2, :] * jnp.exp(top_own - top_here) + sidestat[4:5, :] * jnp.exp(
        top_sib - top_here
    )
    my_stat[2:3, :] = sidestat[2:3, :] + sidestat[5:6, :]

    for dz, dy in peers:
        k = dz * nb + dy
        start(my_stat, my_stat, ss_send.at[k], ss_recv.at[k], peer(dz, dy))

    for k, top in enumerate([top_own, top_sib]):
        colstat[k : k + 1, :] = jnp.exp(top - top_here)

    def query_part(i):
        tall = []
        for k, part, names in sides:
            softs, picks = [], []
            for g in range(2):
                at = span(i + g)
                hit = names == tbuf[i + g][0:1, :]
                soft = ebuf[part, at] * colstat[k : k + 1, at]
                softs.append(jnp.where(hit, 0.0, soft).astype(BF16))
                picks.append(jnp.where(hit, 1.0, 0.0).astype(BF16))
            tall.append(jnp.concatenate(softs + picks, axis=1))
        parts = lax.dot_general(
            jnp.concatenate(tall, axis=0),
            pbuf[...],
            (((0,), (0,)), ((), ())),
            preferred_element_type=F32,
        )
        for g in range(2):
            qsoft[i + g] = parts[g * LANES : g * LANES + rows].astype(BF16)
            qhit[i + g] = parts[(2 + g) * LANES : (2 + g) * LANES + rows].astype(BF16)

    repeat(nr // 2, lambda g: query_part(g * 2))

    for dz, dy in peers:
        k = dz * nb + dy
        arrive(
            stat.at[member((na - dz) % na, (nb - dy) % nb)], ss_send.at[k], ss_recv.at[k]
        )

    top = stat[0, 0:1, :]
    for i in range(1, nr):
        top = jnp.maximum(top, stat[i, 0:1, :])
    summed = jnp.zeros_like(top)
    positive = jnp.zeros_like(top)
    for i in range(nr):
        summed += stat[i, 1:2, :] * jnp.exp(stat[i, 0:1, :] - top)
        positive += stat[i, 2:3, :]
    totals = top + jnp.log(summed)
    sidestat[6:7, :] = jnp.exp(top_own - totals)
    sidestat[7:8, :] = jnp.exp(top_sib - totals)

    colstat[0:1, :] = jnp.exp(top_here - totals)
    colstat[1:2, :] = jnp.exp(positive - totals) - 1.0

    def query_scale(i):
        factors = jnp.transpose(colstat[:, span(i)])[:rows]
        part = qsoft[i].astype(F32) * factors[:, 0:1] + qhit[i].astype(F32) * factors[:, 1:2]
        qpart[i] = (part * inv_temp).astype(BF16)

    def part_at(dz, dy):
        return qpart.at[member(dz, dy)]

    def piece_of(ref, h):
        return ref.at[pl.ds(*pieces[h])]

    for dz in range(1, na):
        first = wrap(zh + dz, na) * nb

        repeat(nb, lambda g: query_scale(first + g))
        for dy in range(1, nb):
            k = dz * nb + dy
            for h in range(steps):
                start(
                    piece_of(part_at(dz, dy), h),
                    piece_of(qy_in.at[k], h),
                    gy_send.at[k, h],
                    gy_recv.at[k, h],
                    peer(0, dy),
                )

    def update(k, xx):
        core = 1 - co if k else co
        base = k * half + xx * 2 * rows
        part = pl.ds(pl.multiple_of(base, 16), 2 * rows)
        names = jnp.concatenate(
            [down + ((zh * 4 + j * 2 + core) * (nb * 2) + yy * 2 + xx) * rows for j in range(2)],
            axis=0,
        )

        def make_delta(i):
            soft = ebuf[part, span(i)] * sidestat[6 + k : 7 + k, span(i)]
            hit = names == tbuf[i][0:1, :]
            dbuf[part, span(i)] = (soft - jnp.where(hit, 1.0, 0.0)).astype(BF16)

        repeat(nr, make_delta)
        return (
            jnp.dot(
                dbuf[part, :],
                qbuf[...],
                preferred_element_type=F32,
            )
            * inv_temp
        )

    def side(ref, xx):
        return ref.at[pl.ds(pl.multiple_of(xx * 2 * rows, 16), 2 * rows)]

    def block(ref, zl, xx):
        return ref.at[pl.ds(pl.multiple_of((xx * 2 + zl) * rows, 16), rows)]

    order = [(1, 1), (0, 1), (1, 0), (0, 0)]

    def at_order(k):
        dz, dx = order[k]
        return (1 - zl if dz else zl, 1 - xx if dx else xx)

    def to_sib(ks):
        for k in ks:
            start(
                block(psib_out, *at_order(k)),
                block(psib_in, *at_order(k)),
                gs_send.at[k],
                gs_recv.at[k],
                sib,
            )

    side(psib_out, 1 - xx)[...] = update(1, 1 - xx).astype(BF16)
    to_sib([0, 1])
    side(pacc, 1 - xx)[...] = update(0, 1 - xx)

    def piece(k, h=None):
        mine, came = block(pacc, *at_order(k)), block(psib_in, *at_order(k))
        if h is not None:
            mine, came = piece_of(mine, h), piece_of(came, h)
        return mine[...] + came[...].astype(F32)

    def sib_arrive(k):
        arrive(block(psib_in, *at_order(k)), gs_send.at[k], gs_recv.at[k])

    sib_arrive(0)
    px_out[0] = piece(0).astype(BF16)
    for h in range(steps):
        start(
            piece_of(px_out.at[0], h),
            piece_of(px_in.at[0], h),
            gp_send.at[0, h],
            gp_recv.at[0, h],
            xnb,
        )
    for dz in range(1, na):
        for h in range(steps):
            total = piece_of(part_at(dz, 0), h)[...].astype(F32)
            for dy in range(1, nb):
                k = dz * nb + dy
                arrive(piece_of(qy_in.at[k], h), gy_send.at[k, h], gy_recv.at[k, h])
                total += piece_of(qy_in.at[k], h)[...].astype(F32)
            piece_of(qz_out.at[dz], h)[...] = total.astype(BF16)
            start(
                piece_of(qz_out.at[dz], h),
                piece_of(qz_in.at[dz], h),
                gz_send.at[dz, h],
                gz_recv.at[dz, h],
                peer(dz, 0),
            )
    repeat(nb, lambda g: query_scale(zh * nb + g))
    for dy in range(1, nb):
        start(part_at(0, dy), qy_in.at[dy], gy_send.at[dy, 0], gy_recv.at[dy, 0], peer(0, dy))

    side(psib_out, xx)[...] = update(1, xx).astype(BF16)
    to_sib([2, 3])
    side(pacc, xx)[...] = update(0, xx)
    sib_arrive(1)
    px_out[1] = piece(1).astype(BF16)
    sib_arrive(2)
    for h in range(steps):
        came = piece_of(px_in.at[0], h)
        arrive(came, gp_send.at[0, h], gp_recv.at[0, h])
        out = piece_of(pz_out, h)
        out[...] = (piece(2, h) + came[...].astype(F32)).astype(BF16)
        start(out, piece_of(pz_in, h), gp_send.at[2, h], gp_recv.at[2, h], znb)
        if h == 0:
            start(px_out.at[1], px_in.at[1], gp_send.at[1, 0], gp_recv.at[1, 0], xnb)

    q_unit, q_len = unit_rows(q_ref[...])
    p_unit, p_len = unit_rows(p_ref[...])
    losses = totals - positive
    picked = jnp.zeros((1, LANES), F32)
    for i in range(nr):
        picked = jnp.where(me_r == i, losses[:, i * LANES : (i + 1) * LANES], picked)
    loss_ref[...] = picked[:, :rows]

    grad = part_at(0, 0)[...].astype(F32)
    for dy in range(1, nb):
        arrive(qy_in.at[dy], gy_send.at[dy, 0], gy_recv.at[dy, 0])
        grad += qy_in[dy].astype(F32)
    for dz in range(1, na):
        for h in range(steps):
            arrive(piece_of(qz_in.at[dz], h), gz_send.at[dz, h], gz_recv.at[dz, h])
        grad += qz_in[dz].astype(F32)
    qg_ref[...] = unit_back(q_unit, q_len, grad)
    save_q = pltpu.make_async_copy(qg_ref, qg_hbm, io_sem.at[2])
    save_q.start()

    sib_arrive(3)
    arrive(px_in.at[1], gp_send.at[1, 0], gp_recv.at[1, 0])
    grad = piece(3) + px_in[1].astype(F32)
    for h in range(steps):
        arrive(piece_of(pz_in, h), gp_send.at[2, h], gp_recv.at[2, h])
    grad += pz_in[...].astype(F32)
    pg_ref[...] = unit_back(p_unit, p_len, grad)
    save_p = pltpu.make_async_copy(pg_ref, pg_hbm, io_sem.at[3])
    save_p.start()

    for copy in sent:
        copy.wait_send()
    save_q.wait()
    save_p.wait()


def deliver(a_in, b_in, c_in, a_out, b_out, c_out):
    a_out[...] = a_in[...]
    b_out[...] = b_in[...]
    c_out[...] = c_in[...]


def local(na, nb, queries, passages, positives, inv_temp):
    rows, width = queries.shape
    nr = na * nb
    lanes = nr * LANES
    steps = len(cut(rows))
    block = (rows, width)
    vmem = pl.BlockSpec(memory_space=pltpu.VMEM)
    smem = pl.BlockSpec(memory_space=pltpu.SMEM)
    anywhere = pl.BlockSpec(memory_space=pl.ANY)
    dma = pltpu.SemaphoreType.DMA
    shapes = (
        jax.ShapeDtypeStruct((1, rows), F32),
        jax.ShapeDtypeStruct(block, BF16),
        jax.ShapeDtypeStruct(block, BF16),
    )
    made = pl.pallas_call(
        functools.partial(kernel, na, nb),
        out_shape=shapes,
        in_specs=[smem, vmem, anywhere, anywhere],
        out_specs=(vmem, anywhere, anywhere),
        scratch_shapes=[
            pltpu.VMEM(block, BF16),
            pltpu.VMEM(block, BF16),
            pltpu.VMEM(block, BF16),
            pltpu.VMEM(block, BF16),
            pltpu.VMEM((lanes, width), BF16),
            pltpu.VMEM((COLS * rows, width), BF16),
            pltpu.VMEM((nr, 8, LANES), jnp.int32),
            pltpu.VMEM((COLS * rows, lanes), F32),
            pltpu.VMEM((COLS * rows, lanes), BF16),
            pltpu.VMEM((nr, 8, lanes), F32),
            pltpu.VMEM((8, lanes), F32),
            pltpu.VMEM((8, lanes), F32),
            pltpu.VMEM((nr, *block), BF16),
            pltpu.VMEM((nr, *block), BF16),
            pltpu.VMEM((COLS * rows // 2, width), F32),
            pltpu.VMEM((COLS * rows // 2, width), BF16),
            pltpu.VMEM((COLS * rows // 2, width), BF16),
            pltpu.VMEM((2, *block), BF16),
            pltpu.VMEM((2, *block), BF16),
            pltpu.VMEM(block, BF16),
            pltpu.VMEM(block, BF16),
            pltpu.VMEM((nr, *block), BF16),
            pltpu.VMEM((nr, *block), BF16),
            pltpu.VMEM((na, *block), BF16),
            pltpu.VMEM((na, *block), BF16),
            dma((4,)),
            dma((7, steps)),
            dma((7, steps)),
            dma((nr, steps)),
            dma((nr, steps)),
            dma((nr,)),
            dma((nr,)),
            dma((nr,)),
            dma((nr,)),
            dma((4,)),
            dma((4,)),
            dma((3, steps)),
            dma((3, steps)),
            dma((nr, steps)),
            dma((nr, steps)),
            dma((na, steps)),
            dma((na, steps)),
        ],
        compiler_params=pltpu.CompilerParams(
            collective_id=0, has_side_effects=True, vmem_limit_bytes=56 * 1024 * 1024
        ),
    )(inv_temp.reshape(1, 1), positives, queries, passages)
    loss, qg, pg = pl.pallas_call(
        deliver,
        out_shape=shapes,
        in_specs=[vmem] * 3,
        out_specs=(vmem,) * 3,
        compiler_params=pltpu.CompilerParams(vmem_limit_bytes=56 * 1024 * 1024),
    )(*made)
    return (loss.reshape(rows), qg, pg)


def solution(mesh):
    na = mesh.shape["pb"] // 4
    nb = mesh.shape["pa"] // 2
    return jax.shard_map(
        functools.partial(local, na, nb),
        mesh=mesh,
        in_specs=(P(("pb", "pa"), None), P(("pb", "pa"), None), P("pb"), P()),
        out_specs=(P(("pb", "pa")), P(("pb", "pa"), None), P(("pb", "pa"), None)),
        check_vma=False,
    )
```

```python
import functools

import jax
import jax.numpy as jnp
from jax import lax
from jax.experimental import pallas as pl
from jax.experimental.pallas import tpu as pltpu
from jax.sharding import PartitionSpec as P

MESH = pl.DeviceIdType.MESH
F32 = jnp.float32
BF16 = jnp.bfloat16
LANES = 128
COLS = 8


def unit_rows(values):
    wide = values.astype(F32)
    length = jnp.sqrt(jnp.sum(wide * wide, axis=1, keepdims=True))
    return (wide / length, length)


def unit_back(unit, length, grad):
    along = jnp.sum(unit * grad, axis=1, keepdims=True)
    return ((grad - unit * along) / length).astype(BF16)


def cut(rows):
    first = 16
    second = (rows - first) // 2 // 16 * 16
    return [(0, first), (first, second), (first + second, rows - first - second)]


def repeat(count, body):
    if count <= 4:
        for k in range(count):
            body(k)
    else:

        @pl.loop(0, count)
        def _(k):
            body(k)


def kernel(
    na,
    nb,
    temp_ref,
    tgt_ref,
    q_hbm,
    p_hbm,
    loss_ref,
    qg_hbm,
    pg_hbm,
    q_ref,
    p_ref,
    qg_ref,
    pg_ref,
    qbuf,
    pbuf,
    tbuf,
    ebuf,
    dbuf,
    stat,
    sidestat,
    colstat,
    qsoft,
    qhit,
    pacc,
    psib_out,
    psib_in,
    px_out,
    px_in,
    pz_out,
    pz_in,
    qpart,
    qy_in,
    qz_out,
    qz_in,
    io_sem,
    ps_send,
    ps_recv,
    qs_send,
    qs_recv,
    ts_send,
    ts_recv,
    ss_send,
    ss_recv,
    gs_send,
    gs_recv,
    gp_send,
    gp_recv,
    gy_send,
    gy_recv,
    gz_send,
    gz_recv,
):
    rows = q_ref.shape[0]
    width = q_ref.shape[1]
    nr = na * nb
    pieces = cut(rows)
    steps = len(pieces)
    pb = lax.axis_index("pb")
    pa = lax.axis_index("pa")
    zh, zl, co = pb // 4, (pb // 2) % 2, pb % 2
    yy, xx = pa // 2, pa % 2

    def dev(zh, zl, co, yy, xx):
        return (zh * 4 + zl * 2 + co, yy * 2 + xx)

    def wrap(v, n):
        return lax.rem(v, n)

    sib = dev(zh, zl, 1 - co, yy, xx)
    xnb = dev(zh, zl, co, yy, 1 - xx)
    znb = dev(zh, 1 - zl, co, yy, xx)

    def peer(dz, dy):
        return dev(wrap(zh + dz, na), zl, co, wrap(yy + dy, nb), xx)

    peers = [(dz, dy) for dz in range(na) for dy in range(nb) if dz or dy]

    barrier = pltpu.get_barrier_semaphore()
    for other in [sib, xnb, znb] + [peer(dz, dy) for dz, dy in peers]:
        pl.semaphore_signal(barrier, inc=1, device_id=other, device_id_type=MESH)
    load_q = pltpu.make_async_copy(q_hbm, q_ref, io_sem.at[0])
    load_p = pltpu.make_async_copy(p_hbm, p_ref, io_sem.at[1])
    load_q.start()
    load_p.start()

    def member(dz, dy):
        return wrap(zh + dz, na) * nb + wrap(yy + dy, nb)

    def pslot(far, zl, xx, h=None):
        base = (far * 4 + xx * 2 + zl) * rows
        if h is None:
            return pbuf.at[pl.ds(pl.multiple_of(base, 16), rows)]
        return pbuf.at[pl.ds(pl.multiple_of(base + pieces[h][0], 16), pieces[h][1])]

    def qslot(dz, dy, h=None):
        base = member(dz, dy) * LANES
        if h is None:
            return qbuf.at[pl.ds(pl.multiple_of(base, LANES), rows)]
        return qbuf.at[pl.ds(pl.multiple_of(base + pieces[h][0], 16), pieces[h][1])]

    def tslot(dz, dy):
        return tbuf.at[member(dz, dy)]

    def move(src, dst, send, recv, to):
        return pltpu.make_async_remote_copy(
            src_ref=src,
            dst_ref=dst,
            send_sem=send,
            recv_sem=recv,
            device_id=to,
            device_id_type=MESH,
        )

    sent = []

    def start(src, dst, send, recv, to):
        copy = move(src, dst, send, recv, to)
        copy.start()
        sent.append(copy)

    def arrive(dst, send, recv):
        move(dst, dst, send, recv, sib).wait_recv()

    def clear(i):
        base = i * LANES + rows
        qbuf[pl.ds(pl.multiple_of(base, 16), LANES - rows), :] = jnp.zeros(
            (LANES - rows, width), BF16
        )

    repeat(nr, clear)

    positives = tgt_ref[...].reshape(1, -1)
    picked = jnp.zeros((1, rows), jnp.int32)
    for k in range(nb * 2):
        picked = jnp.where(pa == k, positives[:, k * rows : (k + 1) * rows], picked)
    me_r = member(0, 0)
    tbuf[me_r] = jnp.full((8, LANES), -1, jnp.int32)
    tbuf[me_r, 0:1, 0:rows] = picked

    load_q.wait()
    q_unit, _ = unit_rows(q_ref[...])
    qslot(0, 0)[...] = q_unit.astype(BF16)
    load_p.wait()
    p_unit, _ = unit_rows(p_ref[...])
    pslot(0, zl, xx)[...] = p_unit.astype(BF16)
    pl.semaphore_wait(barrier, 3 + len(peers))

    def send_p(k, zl, xx, to, h=None):
        far = 1 if k in (2, 4, 5, 6) else 0
        at = (k, h or 0)
        start(pslot(0, zl, xx, h), pslot(far, zl, xx, h), ps_send.at[at], ps_recv.at[at], to)

    def take_p(k, zl, xx, h=None):
        far = 1 if k in (2, 4, 5, 6) else 0
        at = (k, h or 0)
        arrive(pslot(far, zl, xx, h), ps_send.at[at], ps_recv.at[at])

    def send_q(dz, dy, slot, to, h=None):
        at = (dz * nb + dy, h or 0)
        start(slot, slot, qs_send.at[at], qs_recv.at[at], to)

    def take_q(dz, dy, h=None):
        at = (dz * nb + dy, h or 0)
        slot = qslot((na - dz) % na, (nb - dy) % nb, h)
        arrive(slot, qs_send.at[at], qs_recv.at[at])

    for h in range(steps):
        send_p(0, zl, xx, znb, h)
        for dz in range(1, na):
            send_q(dz, 0, qslot(0, 0, h), peer(dz, 0), h)
    for dy in range(1, nb):
        send_q(0, dy, qslot(0, 0), peer(0, dy))
    send_p(1, zl, xx, xnb)
    send_p(2, zl, xx, sib)
    for dz, dy in peers:
        k = dz * nb + dy
        start(tslot(0, 0), tslot(0, 0), ts_send.at[k], ts_recv.at[k], peer(dz, dy))

    def pass_p(h):
        take_p(0, 1 - zl, xx, h)
        send_p(3, 1 - zl, xx, xnb, h)

    def pass_q(h):
        for dz in range(1, na):
            take_q(dz, 0, h)
            for dy in range(1, nb):
                send_q(dz, dy, qslot(na - dz, 0, h), peer(0, dy), h)

    pass_p(0)
    pass_q(0)
    for h in range(1, steps):
        pass_p(h)
    for h in range(1, steps):
        pass_q(h)
    send_p(4, 1 - zl, xx, sib)
    take_p(1, zl, 1 - xx)
    send_p(5, zl, 1 - xx, sib)
    for h in range(steps):
        take_p(3, 1 - zl, 1 - xx, h)
        send_p(6, 1 - zl, 1 - xx, sib, h)
    for dz, dy in peers:
        k = dz * nb + dy
        arrive(tslot((na - dz) % na, (nb - dy) % nb), ts_send.at[k], ts_recv.at[k])

    inv_temp = temp_ref[0, 0]
    count = COLS * rows
    half = count // 2
    my_stat = stat.at[me_r]
    down = lax.broadcasted_iota(jnp.int32, (rows, LANES), 0)

    def ids(core):
        blocks = [
            down + ((zh * 4 + (j % 2) * 2 + core) * (nb * 2) + yy * 2 + j // 2) * rows
            for j in range(COLS // 2)
        ]
        return jnp.concatenate(blocks, axis=0)

    own_half = pl.ds(0, half)
    sib_half = pl.ds(half, half)
    sides = [(0, own_half, ids(co)), (1, sib_half, ids(1 - co))]

    def span(i, n=1):
        if isinstance(i, int):
            return pl.ds(i * LANES, n * LANES)
        return pl.ds(pl.multiple_of(i * LANES, LANES), n * LANES)

    def forward(side, i):
        k, part, names = sides[side]
        both = (
            lax.dot_general(
                pbuf[part, :],
                qbuf[span(i, 2), :],
                (((1,), (1,)), ((), ())),
                preferred_element_type=F32,
            )
            * inv_temp
        )
        for g in range(2):
            logits = both[:, g * LANES : (g + 1) * LANES]
            biggest = jnp.max(logits, axis=0, keepdims=True)
            powers = jnp.exp(logits - biggest)
            at = span(i + g)
            ebuf[part, at] = powers
            hit = names == tbuf[i + g][0:1, :]
            sidestat[3 * k : 3 * k + 1, at] = biggest
            sidestat[3 * k + 1 : 3 * k + 2, at] = jnp.sum(powers, axis=0, keepdims=True)
            sidestat[3 * k + 2 : 3 * k + 3, at] = jnp.sum(
                jnp.where(hit, logits, 0.0), axis=0, keepdims=True
            )

    def forward_all(side, dz):
        first = wrap(zh + (na - dz), na) * nb
        repeat(nb // 2, lambda g: forward(side, first + g * 2))

    for dy in range(1, nb):
        take_q(0, dy)
    forward_all(0, 0)
    for dz in range(1, na):
        for dy in range(1, nb):
            for h in range(steps):
                take_q(dz, dy, h)
        forward_all(0, dz)
    take_p(2, zl, xx)
    take_p(4, 1 - zl, xx)
    take_p(5, zl, 1 - xx)
    for h in range(steps):
        take_p(6, 1 - zl, 1 - xx, h)
    for dz in range(na):
        forward_all(1, dz)

    top_own, top_sib = sidestat[0:1, :], sidestat[3:4, :]
    top_here = jnp.maximum(top_own, top_sib)
    my_stat[0:1, :] = top_here
    my_stat[1:2, :] = sidestat[1:2, :] * jnp.exp(top_own - top_here) + sidestat[4:5, :] * jnp.exp(
        top_sib - top_here
    )
    my_stat[2:3, :] = sidestat[2:3, :] + sidestat[5:6, :]

    for dz, dy in peers:
        k = dz * nb + dy
        start(my_stat, my_stat, ss_send.at[k], ss_recv.at[k], peer(dz, dy))

    for k, top in enumerate([top_own, top_sib]):
        colstat[k : k + 1, :] = jnp.exp(top - top_here)

    def query_part(i):
        tall = []
        for k, part, names in sides:
            softs, picks = [], []
            for g in range(2):
                at = span(i + g)
                hit = names == tbuf[i + g][0:1, :]
                soft = ebuf[part, at] * colstat[k : k + 1, at]
                softs.append(jnp.where(hit, 0.0, soft).astype(BF16))
                picks.append(jnp.where(hit, 1.0, 0.0).astype(BF16))
            tall.append(jnp.concatenate(softs + picks, axis=1))
        parts = lax.dot_general(
            jnp.concatenate(tall, axis=0),
            pbuf[...],
            (((0,), (0,)), ((), ())),
            preferred_element_type=F32,
        )
        for g in range(2):
            qsoft[i + g] = parts[g * LANES : g * LANES + rows].astype(BF16)
            qhit[i + g] = parts[(2 + g) * LANES : (2 + g) * LANES + rows].astype(BF16)

    repeat(nr // 2, lambda g: query_part(g * 2))

    for dz, dy in peers:
        k = dz * nb + dy
        arrive(
            stat.at[member((na - dz) % na, (nb - dy) % nb)], ss_send.at[k], ss_recv.at[k]
        )

    top = stat[0, 0:1, :]
    for i in range(1, nr):
        top = jnp.maximum(top, stat[i, 0:1, :])
    summed = jnp.zeros_like(top)
    positive = jnp.zeros_like(top)
    for i in range(nr):
        summed += stat[i, 1:2, :] * jnp.exp(stat[i, 0:1, :] - top)
        positive += stat[i, 2:3, :]
    totals = top + jnp.log(summed)
    sidestat[6:7, :] = jnp.exp(top_own - totals)
    sidestat[7:8, :] = jnp.exp(top_sib - totals)

    colstat[0:1, :] = jnp.exp(top_here - totals)
    colstat[1:2, :] = jnp.exp(positive - totals) - 1.0

    def query_scale(i):
        factors = jnp.transpose(colstat[:, span(i)])[:rows]
        part = qsoft[i].astype(F32) * factors[:, 0:1] + qhit[i].astype(F32) * factors[:, 1:2]
        qpart[i] = (part * inv_temp).astype(BF16)

    def part_at(dz, dy):
        return qpart.at[member(dz, dy)]

    def piece_of(ref, h):
        return ref.at[pl.ds(*pieces[h])]

    for dz in range(1, na):
        first = wrap(zh + dz, na) * nb

        repeat(nb, lambda g: query_scale(first + g))
        for dy in range(1, nb):
            k = dz * nb + dy
            for h in range(steps):
                start(
                    piece_of(part_at(dz, dy), h),
                    piece_of(qy_in.at[k], h),
                    gy_send.at[k, h],
                    gy_recv.at[k, h],
                    peer(0, dy),
                )

    def update(k, xx):
        core = 1 - co if k else co
        base = k * half + xx * 2 * rows
        part = pl.ds(pl.multiple_of(base, 16), 2 * rows)
        names = jnp.concatenate(
            [down + ((zh * 4 + j * 2 + core) * (nb * 2) + yy * 2 + xx) * rows for j in range(2)],
            axis=0,
        )

        def make_delta(i):
            soft = ebuf[part, span(i)] * sidestat[6 + k : 7 + k, span(i)]
            hit = names == tbuf[i][0:1, :]
            dbuf[part, span(i)] = (soft - jnp.where(hit, 1.0, 0.0)).astype(BF16)

        repeat(nr, make_delta)
        return (
            jnp.dot(
                dbuf[part, :],
                qbuf[...],
                preferred_element_type=F32,
            )
            * inv_temp
        )

    def side(ref, xx):
        return ref.at[pl.ds(pl.multiple_of(xx * 2 * rows, 16), 2 * rows)]

    def block(ref, zl, xx):
        return ref.at[pl.ds(pl.multiple_of((xx * 2 + zl) * rows, 16), rows)]

    order = [(1, 1), (0, 1), (1, 0), (0, 0)]

    def at_order(k):
        dz, dx = order[k]
        return (1 - zl if dz else zl, 1 - xx if dx else xx)

    def to_sib(ks):
        for k in ks:
            start(
                block(psib_out, *at_order(k)),
                block(psib_in, *at_order(k)),
                gs_send.at[k],
                gs_recv.at[k],
                sib,
            )

    side(psib_out, 1 - xx)[...] = update(1, 1 - xx).astype(BF16)
    to_sib([0, 1])
    side(pacc, 1 - xx)[...] = update(0, 1 - xx)
    side(psib_out, xx)[...] = update(1, xx).astype(BF16)
    to_sib([2, 3])

    def piece(k, h=None):
        mine, came = block(pacc, *at_order(k)), block(psib_in, *at_order(k))
        if h is not None:
            mine, came = piece_of(mine, h), piece_of(came, h)
        return mine[...] + came[...].astype(F32)

    def sib_arrive(k):
        arrive(block(psib_in, *at_order(k)), gs_send.at[k], gs_recv.at[k])

    sib_arrive(0)
    px_out[0] = piece(0).astype(BF16)
    for h in range(steps):
        start(
            piece_of(px_out.at[0], h),
            piece_of(px_in.at[0], h),
            gp_send.at[0, h],
            gp_recv.at[0, h],
            xnb,
        )
    for dz in range(1, na):
        for h in range(steps):
            total = piece_of(part_at(dz, 0), h)[...].astype(F32)
            for dy in range(1, nb):
                k = dz * nb + dy
                arrive(piece_of(qy_in.at[k], h), gy_send.at[k, h], gy_recv.at[k, h])
                total += piece_of(qy_in.at[k], h)[...].astype(F32)
            piece_of(qz_out.at[dz], h)[...] = total.astype(BF16)
            start(
                piece_of(qz_out.at[dz], h),
                piece_of(qz_in.at[dz], h),
                gz_send.at[dz, h],
                gz_recv.at[dz, h],
                peer(dz, 0),
            )
    repeat(nb, lambda g: query_scale(zh * nb + g))
    for dy in range(1, nb):
        start(part_at(0, dy), qy_in.at[dy], gy_send.at[dy, 0], gy_recv.at[dy, 0], peer(0, dy))

    side(pacc, xx)[...] = update(0, xx)
    sib_arrive(1)
    px_out[1] = piece(1).astype(BF16)
    sib_arrive(2)
    for h in range(steps):
        came = piece_of(px_in.at[0], h)
        arrive(came, gp_send.at[0, h], gp_recv.at[0, h])
        out = piece_of(pz_out, h)
        out[...] = (piece(2, h) + came[...].astype(F32)).astype(BF16)
        start(out, piece_of(pz_in, h), gp_send.at[2, h], gp_recv.at[2, h], znb)
        if h == 0:
            start(px_out.at[1], px_in.at[1], gp_send.at[1, 0], gp_recv.at[1, 0], xnb)

    q_unit, q_len = unit_rows(q_ref[...])
    p_unit, p_len = unit_rows(p_ref[...])
    losses = totals - positive
    picked = jnp.zeros((1, LANES), F32)
    for i in range(nr):
        picked = jnp.where(me_r == i, losses[:, i * LANES : (i + 1) * LANES], picked)
    loss_ref[...] = picked[:, :rows]

    grad = part_at(0, 0)[...].astype(F32)
    for dy in range(1, nb):
        arrive(qy_in.at[dy], gy_send.at[dy, 0], gy_recv.at[dy, 0])
        grad += qy_in[dy].astype(F32)
    for dz in range(1, na):
        for h in range(steps):
            arrive(piece_of(qz_in.at[dz], h), gz_send.at[dz, h], gz_recv.at[dz, h])
        grad += qz_in[dz].astype(F32)
    qg_ref[...] = unit_back(q_unit, q_len, grad)
    save_q = pltpu.make_async_copy(qg_ref, qg_hbm, io_sem.at[2])
    save_q.start()

    sib_arrive(3)
    arrive(px_in.at[1], gp_send.at[1, 0], gp_recv.at[1, 0])
    grad = piece(3) + px_in[1].astype(F32)
    for h in range(steps):
        arrive(piece_of(pz_in, h), gp_send.at[2, h], gp_recv.at[2, h])
    grad += pz_in[...].astype(F32)
    pg_ref[...] = unit_back(p_unit, p_len, grad)
    save_p = pltpu.make_async_copy(pg_ref, pg_hbm, io_sem.at[3])
    save_p.start()

    for copy in sent:
        copy.wait_send()
    save_q.wait()
    save_p.wait()


def deliver(a_in, b_in, c_in, a_out, b_out, c_out):
    a_out[...] = a_in[...]
    b_out[...] = b_in[...]
    c_out[...] = c_in[...]


def local(na, nb, queries, passages, positives, inv_temp):
    rows, width = queries.shape
    nr = na * nb
    lanes = nr * LANES
    steps = len(cut(rows))
    block = (rows, width)
    vmem = pl.BlockSpec(memory_space=pltpu.VMEM)
    smem = pl.BlockSpec(memory_space=pltpu.SMEM)
    anywhere = pl.BlockSpec(memory_space=pl.ANY)
    dma = pltpu.SemaphoreType.DMA
    shapes = (
        jax.ShapeDtypeStruct((1, rows), F32),
        jax.ShapeDtypeStruct(block, BF16),
        jax.ShapeDtypeStruct(block, BF16),
    )
    made = pl.pallas_call(
        functools.partial(kernel, na, nb),
        out_shape=shapes,
        in_specs=[smem, vmem, anywhere, anywhere],
        out_specs=(vmem, anywhere, anywhere),
        scratch_shapes=[
            pltpu.VMEM(block, BF16),
            pltpu.VMEM(block, BF16),
            pltpu.VMEM(block, BF16),
            pltpu.VMEM(block, BF16),
            pltpu.VMEM((lanes, width), BF16),
            pltpu.VMEM((COLS * rows, width), BF16),
            pltpu.VMEM((nr, 8, LANES), jnp.int32),
            pltpu.VMEM((COLS * rows, lanes), F32),
            pltpu.VMEM((COLS * rows, lanes), BF16),
            pltpu.VMEM((nr, 8, lanes), F32),
            pltpu.VMEM((8, lanes), F32),
            pltpu.VMEM((8, lanes), F32),
            pltpu.VMEM((nr, *block), BF16),
            pltpu.VMEM((nr, *block), BF16),
            pltpu.VMEM((COLS * rows // 2, width), F32),
            pltpu.VMEM((COLS * rows // 2, width), BF16),
            pltpu.VMEM((COLS * rows // 2, width), BF16),
            pltpu.VMEM((2, *block), BF16),
            pltpu.VMEM((2, *block), BF16),
            pltpu.VMEM(block, BF16),
            pltpu.VMEM(block, BF16),
            pltpu.VMEM((nr, *block), BF16),
            pltpu.VMEM((nr, *block), BF16),
            pltpu.VMEM((na, *block), BF16),
            pltpu.VMEM((na, *block), BF16),
            dma((4,)),
            dma((7, steps)),
            dma((7, steps)),
            dma((nr, steps)),
            dma((nr, steps)),
            dma((nr,)),
            dma((nr,)),
            dma((nr,)),
            dma((nr,)),
            dma((4,)),
            dma((4,)),
            dma((3, steps)),
            dma((3, steps)),
            dma((nr, steps)),
            dma((nr, steps)),
            dma((na, steps)),
            dma((na, steps)),
        ],
        compiler_params=pltpu.CompilerParams(
            collective_id=0, has_side_effects=True, vmem_limit_bytes=56 * 1024 * 1024
        ),
    )(inv_temp.reshape(1, 1), positives, queries, passages)
    loss, qg, pg = pl.pallas_call(
        deliver,
        out_shape=shapes,
        in_specs=[vmem] * 3,
        out_specs=(vmem,) * 3,
        compiler_params=pltpu.CompilerParams(vmem_limit_bytes=56 * 1024 * 1024),
    )(*made)
    return (loss.reshape(rows), qg, pg)


def solution(mesh):
    na = mesh.shape["pb"] // 4
    nb = mesh.shape["pa"] // 2
    return jax.shard_map(
        functools.partial(local, na, nb),
        mesh=mesh,
        in_specs=(P(("pb", "pa"), None), P(("pb", "pa"), None), P("pb"), P()),
        out_specs=(P(("pb", "pa")), P(("pb", "pa"), None), P(("pb", "pa"), None)),
        check_vma=False,
    )
```
